32 devices in a mesh: seq: 4 (over y, x), section: 4 (over z), mp: 2 (over core).
Axes of the slice: x: 2, y: 2, z: 4, core: 2. Of those that a mesh axis runs over, the one named last changes fastest.
Arguments:
- enc_rows: bfloat16 [4, 1024, 512], P('section', 'seq'), may hold values from -6 to 6
- proj_weight: bfloat16 [512, 8192], P(None, 'mp'), may hold values from -0.25 to 0.25
- row_owner: int32 [4, 1024], P('section', 'seq'), may hold values from -1 to 3, as said below
- grad_in: bfloat16 [4, 1024, 8192], P('section', 'seq', 'mp'), may hold values from -3 to 3
- adapter_gain: float32 [4, 8192], P('section', 'mp'), may hold values from 0.25 to 1.75
- adapter_down: bfloat16 [4, 64, 8192], P('section', None, 'mp'), may hold values from -0.375 to 0.375
- adapter_up: bfloat16 [4, 64, 8192], P('section', None, 'mp'), may hold values from -0.0625 to 0.0625
Outputs:
- soft_tokens: bfloat16 [4, 1024, 8192], P('section', 'seq', 'mp')
- enc_grad: float32 [4, 1024, 512], P('section', 'seq', 'mp')
The draws below stay inside these ranges and needn't reach their ends.
Inputs may be any that keep to these rules, and one draw needn't show every extreme that they name: row_owner[s, r] is the reader device along seq of encoder row r of micro-batch s, or -1 for an empty row. Every reader receives 16 to 256 rows of a micro-batch, and one reader exactly 256. One encoder device holds at most 64 rows for one reader, and exactly 64 for that fullest reader.
All inputs are finite; a program needn't handle non-finite values.
Results may differ from the reference program's by a relative error of at most 0.0061.
Values may be sent and summed in bfloat16 or wider, within the bound.
A program may use at most 64 MiB of HBM per device.

```python
import jax
import jax.numpy as jnp
from jax import lax

D = 8192
G = 512
R = 64
SLOTS = 256
TICKS = 2
SECTIONS = 4
CAP = 64
ROWS = 1024
N_SEQ = 4
N_SECTION = 4


def owner_block(key):
    subkeys = jax.random.split(key, 5)
    extra_span = SLOTS - 16
    factor_one = jax.random.randint(subkeys[0], (N_SEQ,), 0, extra_span + 1)
    factor_two = jax.random.randint(subkeys[1], (N_SEQ,), 0, extra_span + 1)
    reader_loads = 16 + factor_one * factor_two // extra_span
    fullest = jax.random.randint(subkeys[2], (), 0, N_SEQ)
    readers = jnp.arange(N_SEQ, dtype=jnp.int32)
    reader_loads = jnp.where(readers == fullest, SLOTS, reader_loads).astype(jnp.int32)
    reader_order = jax.random.permutation(subkeys[3], N_SEQ).astype(jnp.int32)
    ordered = reader_loads[reader_order]
    run_ends = jnp.cumsum(ordered)
    position = jnp.arange(N_SEQ * SLOTS, dtype=jnp.int32)
    run_index = jnp.sum((position[:, None] >= run_ends[None, :]).astype(jnp.int32), axis=1)
    owners = jnp.where(run_index < N_SEQ, reader_order[jnp.minimum(run_index, N_SEQ - 1)], -1)
    layout = owners.reshape(SLOTS, N_SEQ).T
    shuffles = jax.vmap(lambda subkey: jax.random.permutation(subkey, SLOTS))(jax.random.split(subkeys[4], N_SEQ))
    layout = jnp.take_along_axis(layout, shuffles, axis=1)
    return layout.reshape(N_SEQ * SLOTS).astype(jnp.int32)


def draw_row_owner(key, part):
    return jax.vmap(owner_block)(jax.random.split(key, N_SECTION))


def level_of(key, shape, shards, low, top_value):
    loudness, own = 1.0, jax.random.fold_in(key, 6)
    for axis_at, parts in shards:
        draws = jnp.exp(jax.random.uniform(jax.random.fold_in(own, axis_at), (parts,), jnp.float32, low / len(shards), top_value / len(shards)))
        loudness = loudness * jnp.repeat(draws, shape[axis_at] // parts).reshape([-1 if axis == axis_at else 1 for axis in range(len(shape))])
    return loudness


def bell_draw(key, shape, scale, bound, cuts=(), kind=jnp.bfloat16):
    entries = scale * jax.random.normal(key, shape, jnp.float32)
    if cuts:
        entries = entries * level_of(key, shape, cuts, -0.22, 0.18)
    return jnp.clip(entries, -bound, bound).astype(kind)


def setup_inputs(seed: int = 0) -> dict:
    streams_of = jax.random.split(jax.random.key(seed), 8)
    enc_rows = bell_draw(streams_of[0], (SECTIONS, ROWS, G), 1.0, 6.0, ((0, 4), (1, 4)))
    proj_weight = bell_draw(streams_of[1], (G, D), G ** -0.5, 0.25, ((1, 2),))
    row_owner = draw_row_owner(jax.random.fold_in(streams_of[7], 71), 0)
    grad_in = bell_draw(streams_of[3], (SECTIONS, ROWS, D), 0.5, 3.0, ((0, 4), (1, 4), (2, 2)))
    adapter_gain = jnp.clip(1.0 + 0.15 * jax.random.normal(streams_of[4], (SECTIONS, D), jnp.float32), 0.25, 1.75)
    adapter_down = bell_draw(streams_of[5], (SECTIONS, R, D), (4 * R) ** -0.5, 0.375, ((0, 4), (2, 2)))
    adapter_up = bell_draw(streams_of[6], (SECTIONS, R, D), D ** -0.5, 0.0625, ((0, 4), (2, 2)))
    return dict(enc_rows=enc_rows, proj_weight=proj_weight, row_owner=row_owner, grad_in=grad_in, adapter_gain=adapter_gain, adapter_down=adapter_down, adapter_up=adapter_up)


def route_block(owners):
    readers = jnp.arange(N_SEQ, dtype=jnp.int32)
    matches = (owners[:, None] == readers[None, :]).astype(jnp.int32)
    before = jnp.cumsum(matches, axis=0) - matches
    return jnp.sum(matches * before, axis=1).astype(jnp.int32)


def adapter_back(carried, gain_row, down_rows, up_rows):
    reduced = jnp.dot(carried, up_rows.T, preferred_element_type=jnp.float32).astype(jnp.bfloat16)
    spread = jnp.dot(reduced, down_rows, preferred_element_type=jnp.float32)
    return (carried.astype(jnp.float32) + gain_row[None, :] * spread).astype(jnp.bfloat16)


def reference(enc_rows, proj_weight, row_owner, grad_in, adapter_gain, adapter_down, adapter_up):
    def one_segment(home):
        owners = row_owner[home].reshape(N_SEQ, SLOTS)
        order_rank = jax.vmap(route_block)(owners)
        encoder = jnp.arange(N_SEQ, dtype=jnp.int32)[:, None]
        is_valid = owners >= 0
        flat_slot = jnp.where(is_valid, owners * SLOTS + encoder * CAP + order_rank, ROWS).reshape(ROWS).astype(jnp.int32)
        projected = jnp.dot(enc_rows[home], proj_weight, preferred_element_type=jnp.float32).astype(jnp.bfloat16)
        soft_block = jnp.zeros((ROWS, D), jnp.bfloat16).at[flat_slot].set(projected, mode="drop")
        carried = grad_in[(home + TICKS) % SECTIONS]
        for tick_index in range(TICKS + 1):
            layer_index = (home + TICKS - tick_index) % SECTIONS
            carried = adapter_back(carried, adapter_gain[layer_index], adapter_down[layer_index], adapter_up[layer_index])
        picked = jnp.take(carried, jnp.minimum(flat_slot, ROWS - 1), axis=0)
        picked = jnp.where(is_valid.reshape(ROWS)[:, None], picked, jnp.zeros_like(picked))
        row_grads = jnp.dot(picked, proj_weight.T, preferred_element_type=jnp.float32)
        return soft_block, row_grads

    soft_tokens, enc_grad = lax.map(one_segment, jnp.arange(SECTIONS, dtype=jnp.int32))
    return soft_tokens, enc_grad
```

```python
import functools

import jax
import jax.numpy as jnp
from jax import lax
from jax.experimental import pallas as pl
from jax.experimental.pallas import tpu as pltpu
from jax.sharding import PartitionSpec as P

TICKS = 2
MESH = pl.DeviceIdType.MESH
F32, BF16 = jnp.float32, jnp.bfloat16


def times(a, b):
    return jnp.dot(a, b, preferred_element_type=F32)


def times_t(a, b):
    return lax.dot_general(a, b, (((1,), (1,)), ((), ())), preferred_element_type=F32)


def aligned(value, unit):
    return pl.multiple_of(value, unit)


def kernel(
    counts,
    enc_hbm, proj_hbm, owner_hbm, grad_hbm, gain_hbm, down_hbm, up_hbm,
    soft_hbm, out_hbm,
    enc, owner, gain, down, x, w, staged, routed, pick_t, soft,
    part, part_in, low, low_in, late, late_in,
    home, home_in, tail, tail_in, q_own, q_in, m_own, m_in, mix, out,
    load_sem, store_sem, send_sem, recv_sem,
):
    n_q, n_z, n_m = counts
    q, z, m = lax.axis_index("seq"), lax.axis_index("section"), lax.axis_index("mp")
    slots, width = enc.shape
    rank, features = down.shape
    columns = width // n_m
    per = slots // n_q
    share = features // n_q

    def device(dq, dz, dm):
        return (lax.rem(q + dq % n_q, n_q), lax.rem(z + dz % n_z, n_z), lax.rem(m + dm % n_m, n_m))

    used = [0, 0, 0]
    sent = []

    def load(src, dst):
        copy = pltpu.make_async_copy(src, dst, load_sem.at[used[0]])
        used[0] += 1
        copy.start()
        return copy

    def store(src, dst):
        copy = pltpu.make_async_copy(src, dst, store_sem.at[used[1]])
        used[1] += 1
        copy.start()
        return copy

    def send(src, dst, offsets):
        copy = pltpu.make_async_remote_copy(
            src_ref=src, dst_ref=dst,
            send_sem=send_sem.at[used[2]], recv_sem=recv_sem.at[used[2]],
            device_id=device(*offsets), device_id_type=MESH,
        )
        used[2] += 1
        copy.start()
        sent.append(copy)
        return copy

    owner_load = load(owner_hbm, owner)
    enc_load = load(enc_hbm.at[0], enc)
    low_load = load(up_hbm.at[0], w.at[pl.ds(width, rank)])
    grad_load = load(grad_hbm.at[0], x.at[pl.ds(0, slots)])
    gain_load = load(gain_hbm, gain)
    down_load = load(down_hbm.at[0], down)
    proj_loads = [
        load(proj_hbm.at[pl.ds(j * columns, columns)], w.at[pl.ds(j * columns, columns)])
        for j in range(n_m)
    ]

    targets = {(dq, 0, 0) for dq in range(1, n_q)}
    targets |= {(0, dz % n_z, 0) for dz in (1, TICKS, -1)}
    targets |= {(dq, -TICKS % n_z, 0) for dq in range(n_q)}
    targets |= {(0, 0, dm) for dm in range(1, n_m)}
    barrier = pltpu.get_barrier_semaphore()
    for dq, dz, dm in sorted(targets):
        pl.semaphore_signal(barrier, inc=1, device_id=device(-dq, -dz, -dm), device_id_type=MESH)
    pl.semaphore_wait(barrier, len(targets))

    own_share = pl.ds(aligned(q * share, share), share)
    up_rows = [pl.ds(width + tick * rank, rank) for tick in range(TICKS + 1)]
    up_sends = [
        send(up_hbm.at[0, :, own_share], w.at[up_rows[tick], own_share], (0, tick, 0))
        for tick in range(1, TICKS + 1)
    ]

    owner_load.wait()
    owners = owner[...].astype(F32)
    readers = lax.broadcasted_iota(jnp.int32, (max(8, n_q), slots), 0).astype(F32)
    matches = jnp.where(owners == readers, 1.0, 0.0)
    row_at = lax.broadcasted_iota(jnp.int32, (slots, slots), 0)
    column_at = lax.broadcasted_iota(jnp.int32, (slots, slots), 1)
    earlier = jnp.where(row_at < column_at, 1.0, 0.0).astype(BF16)
    before = times(matches.astype(BF16), earlier)
    order_rank = jnp.sum(matches * before, axis=0, keepdims=True)
    target = jnp.where(owners >= 0.0, owners * per + order_rank, -1.0)
    pick = jnp.where(row_at.astype(F32) == target, 1.0, 0.0)
    enc_load.wait()
    staged[...] = times(pick.astype(BF16), enc[...]).astype(BF16)
    own_rows = pl.ds(aligned(q * per, per), per)

    def rows_of(dq):
        return pl.ds(aligned(lax.rem(q + dq, n_q) * per, per), per)

    enc_sends = [
        send(staged.at[rows_of(dq)], routed.at[own_rows], (dq, 0, 0)) for dq in range(1, n_q)
    ]
    routed[own_rows, :] = staged[own_rows, :]
    pick_t[...] = jnp.transpose(pick).astype(BF16)

    grad_load.wait()
    low_load.wait()
    low[...] = times_t(x[pl.ds(0, slots), :], w[up_rows[0], :])
    low_sends = [send(low, low_in.at[dm - 1], (0, 0, dm)) for dm in range(1, n_m)]
    down_load.wait()
    gain_load.wait()
    x[pl.ds(slots, rank), :] = (gain[...] * down[...].astype(F32)).astype(BF16)
    for j in range(n_m):
        proj_loads[j].wait()
        part[j] = times_t(x[...], w[pl.ds(j * columns, columns), :])
    part_sends = [
        send(part.at[lax.rem(m + dm, n_m)], part_in.at[dm - 1], (0, 0, dm)) for dm in range(1, n_m)
    ]

    up_spread = []
    for tick in range(1, TICKS + 1):
        up_sends[tick - 1].wait_recv()
        up_spread += [
            send(w.at[up_rows[tick], own_share], w.at[up_rows[tick], own_share], (dq, 0, 0))
            for dq in range(1, n_q)
        ]

    for copy in low_sends + part_sends:
        copy.wait_recv()
    u_own = low[...]
    sums = part[m]
    for dm in range(1, n_m):
        u_own += low_in[dm - 1]
        sums += part_in[dm - 1]
    u_own = u_own.astype(BF16)
    q_own[...] = sums[slots:]
    home[...] = (sums[:slots] + times(u_own, sums[slots:].astype(BF16))).astype(BF16)
    home_sends = [
        send(home.at[rows_of(dq)], home_in.at[own_rows], (dq, -TICKS, 0)) for dq in range(n_q)
    ]
    q_send = send(q_own, q_in, (0, -1, 0))

    for copy in enc_sends:
        copy.wait_recv()
    stores = []
    tile = min(512, features)
    for start in range(0, features, tile):
        at = pl.ds(start, tile)
        soft[:, at] = times(routed[...], w[pl.ds(0, width), at]).astype(BF16)
        stores.append(store(soft.at[:, at], soft_hbm.at[0, :, at]))

    for copy in up_spread:
        copy.wait_recv()
    late[...] = times_t(x[...], w[pl.ds(width + rank, TICKS * rank), :])
    late_sends = [send(late, late_in.at[dm - 1], (0, 0, dm)) for dm in range(1, n_m)]
    for copy in late_sends:
        copy.wait_recv()
    sums = late[...]
    for dm in range(1, n_m):
        sums += late_in[dm - 1]
    m_own[...] = sums[slots:]
    m_send = send(m_own, m_in, (0, -1, 0))
    tail[...] = (sums[:slots] + times(u_own, sums[slots:].astype(BF16))).astype(BF16)
    tail_sends = [
        send(tail.at[rows_of(dq)], tail_in.at[own_rows], (dq, -TICKS, 0)) for dq in range(n_q)
    ]

    for copy in home_sends:
        copy.wait_recv()
    out[...] = times(pick_t[...], home_in[...])
    q_send.wait_recv()
    m_send.wait_recv()
    mix[pl.ds(0, rank), :] = (
        q_in[...] + times(m_in[...][:, :rank].astype(BF16), q_own[...].astype(BF16))
    ).astype(BF16)
    mix[pl.ds(rank, rank), :] = q_own[...].astype(BF16)
    for copy in tail_sends:
        copy.wait_recv()
    out[...] += times(times(pick_t[...], tail_in[...]).astype(BF16), mix[...])
    stores.append(store(out, out_hbm.at[0]))
    for copy in sent:
        copy.wait_send()
    for copy in stores:
        copy.wait()


def on_device(enc_rows, proj_weight, row_owner, grad_in, adapter_gain, adapter_down, adapter_up):
    counts = tuple(lax.axis_size(axis) for axis in ("seq", "section", "mp"))
    n_q, n_z, n_m = counts
    _, slots, width = enc_rows.shape
    _, rank, features = adapter_down.shape
    columns = width // n_m
    tiles = features // min(512, features)
    messages = TICKS + (n_q - 1) * (1 + TICKS) + 3 * (n_m - 1) + 2 * n_q + 2
    flops = 2 * slots * features * (2 * width + 3 * rank)
    vmem = pltpu.VMEM
    return pl.pallas_call(
        functools.partial(kernel, counts),
        out_shape=(
            jax.ShapeDtypeStruct((1, slots, features), BF16),
            jax.ShapeDtypeStruct((1, slots, columns), F32),
        ),
        in_specs=[pl.BlockSpec(memory_space=pl.ANY)] * 7,
        out_specs=(pl.BlockSpec(memory_space=pl.ANY),) * 2,
        scratch_shapes=[
            vmem((slots, width), BF16),
            vmem((1, slots), jnp.int32),
            vmem((1, features), F32),
            vmem((rank, features), BF16),
            vmem((slots + rank, features), BF16),
            vmem((width + (TICKS + 1) * rank, features), BF16),
            vmem((slots, width), BF16),
            vmem((slots, width), BF16),
            vmem((slots, slots), BF16),
            vmem((slots, features), BF16),
            vmem((n_m, slots + rank, columns), F32),
            vmem((n_m - 1, slots + rank, columns), F32),
            vmem((slots, rank), F32),
            vmem((n_m - 1, slots, rank), F32),
            vmem((slots + rank, TICKS * rank), F32),
            vmem((n_m - 1, slots + rank, TICKS * rank), F32),
            vmem((slots, columns), BF16),
            vmem((slots, columns), BF16),
            vmem((slots, TICKS * rank), BF16),
            vmem((slots, TICKS * rank), BF16),
            vmem((rank, columns), F32),
            vmem((rank, columns), F32),
            vmem((rank, TICKS * rank), F32),
            vmem((rank, TICKS * rank), F32),
            vmem((TICKS * rank, columns), BF16),
            vmem((slots, columns), F32),
            pltpu.SemaphoreType.DMA((6 + n_m,)),
            pltpu.SemaphoreType.DMA((tiles + 1,)),
            pltpu.SemaphoreType.DMA((messages,)),
            pltpu.SemaphoreType.DMA((messages,)),
        ],
        compiler_params=pltpu.CompilerParams(
            collective_id=0, has_side_effects=True, vmem_limit_bytes=48 * 1024 * 1024
        ),
        cost_estimate=pl.CostEstimate(flops=flops, bytes_accessed=12 * 1024 * 1024, transcendentals=0),
    )(enc_rows, proj_weight, row_owner, grad_in, adapter_gain, adapter_down, adapter_up)


def solution(mesh):
    placed = (
        P("section", "seq", None),
        P(None, "mp"),
        P("section", "seq"),
        P("section", "seq", "mp"),
        P("section", "mp"),
        P("section", None, "mp"),
        P("section", None, "mp"),
    )
    return jax.shard_map(
        on_device,
        mesh=mesh,
        in_specs=placed,
        out_specs=(P("section", "seq", "mp"), P("section", "seq", "mp")),
        check_vma=False,
    )
```

```python
import functools

import jax
import jax.numpy as jnp
from jax import lax
from jax.experimental import pallas as pl
from jax.experimental.pallas import tpu as pltpu
from jax.sharding import PartitionSpec as P

TICKS = 2
MESH = pl.DeviceIdType.MESH
F32, BF16 = jnp.float32, jnp.bfloat16


def times(a, b):
    return jnp.dot(a, b, preferred_element_type=F32)


def times_t(a, b):
    return lax.dot_general(a, b, (((1,), (1,)), ((), ())), preferred_element_type=F32)


def aligned(value, unit):
    return pl.multiple_of(value, unit)


def kernel(
    counts, pieces,
    enc_hbm, proj_hbm, owner_hbm, grad_hbm, gain_hbm, down_hbm, up_hbm,
    soft_hbm, out_hbm,
    enc, owner, gain, down, x, w, staged, routed, pick_t, soft,
    part, part_in, low, low_in, late, late_in,
    home, home_in, tail, tail_in, q_own, q_in, m_own, m_in, out,
    load_sem, store_sem, send_sem, recv_sem,
):
    n_q, n_z, n_m = counts
    q, z, m = lax.axis_index("seq"), lax.axis_index("section"), lax.axis_index("mp")
    slots, width = enc.shape
    rank, features = down.shape
    columns = width // n_m
    per = slots // n_q
    share = features // n_q

    def device(dq, dz, dm):
        return (lax.rem(q + dq % n_q, n_q), lax.rem(z + dz % n_z, n_z), lax.rem(m + dm % n_m, n_m))

    used = [0, 0, 0]
    sent = []

    def load(src, dst):
        copy = pltpu.make_async_copy(src, dst, load_sem.at[used[0]])
        used[0] += 1
        copy.start()
        return copy

    def store(src, dst):
        copy = pltpu.make_async_copy(src, dst, store_sem.at[used[1]])
        used[1] += 1
        copy.start()
        return copy

    def send(src, dst, offsets):
        copy = pltpu.make_async_remote_copy(
            src_ref=src, dst_ref=dst,
            send_sem=send_sem.at[used[2]], recv_sem=recv_sem.at[used[2]],
            device_id=device(*offsets), device_id_type=MESH,
        )
        used[2] += 1
        copy.start()
        sent.append(copy)
        return copy

    owner_load = load(owner_hbm, owner)
    enc_load = load(enc_hbm.at[0], enc)
    low_load = load(up_hbm.at[0], w.at[pl.ds(width, rank)])
    grad_load = load(grad_hbm.at[0], x.at[pl.ds(0, slots)])
    gain_load = load(gain_hbm, gain)
    down_load = load(down_hbm.at[0], down)
    proj_loads = [
        load(proj_hbm.at[pl.ds(j * columns, columns)], w.at[pl.ds(j * columns, columns)])
        for j in range(n_m)
    ]

    targets = {(dq, 0, 0) for dq in range(1, n_q)}
    targets |= {(0, 1, 0), (0, -1 % n_z, 0)}
    targets |= {(dq, -TICKS % n_z, 0) for dq in range(n_q)}
    targets |= {(0, 0, dm) for dm in range(1, n_m)}
    barrier = pltpu.get_barrier_semaphore()
    for dq, dz, dm in sorted(targets):
        pl.semaphore_signal(barrier, inc=1, device_id=device(-dq, -dz, -dm), device_id_type=MESH)

    owner_load.wait()
    owners = owner[...].astype(F32)
    readers = lax.broadcasted_iota(jnp.int32, (max(8, n_q), slots), 0).astype(F32)
    matches = jnp.where(owners == readers, 1.0, 0.0)
    row_at = lax.broadcasted_iota(jnp.int32, (slots, slots), 0)
    column_at = lax.broadcasted_iota(jnp.int32, (slots, slots), 1)
    earlier = jnp.where(row_at < column_at, 1.0, 0.0).astype(BF16)
    before = times(matches.astype(BF16), earlier)
    order_rank = jnp.sum(matches * before, axis=0, keepdims=True)
    target = jnp.where(owners >= 0.0, owners * per + order_rank, -1.0)
    pick = jnp.where(row_at.astype(F32) == target, 1.0, 0.0)
    enc_load.wait()
    staged[...] = times(pick.astype(BF16), enc[...]).astype(BF16)
    pl.semaphore_wait(barrier, len(targets))

    piece = share // pieces
    up_rows = [pl.ds(width + tick * rank, rank) for tick in range(TICKS + 1)]

    def piece_at(h):
        return pl.ds(aligned(q * share + h * piece, 128), piece)

    ring = [
        [
            send(up_hbm.at[0, :, piece_at(h)], w.at[up_rows[1], piece_at(h)], (0, 1, 0))
            for h in range(pieces)
        ]
    ] + [[] for _ in range(1, TICKS)]
    spread = [[] for _ in range(TICKS)]

    def pass_on(tick, h):
        ring[tick][h].wait_recv()
        here = w.at[up_rows[tick + 1], piece_at(h)]
        if tick + 1 < TICKS:
            ring[tick + 1].append(send(here, w.at[up_rows[tick + 2], piece_at(h)], (0, 1, 0)))
        spread[tick] += [send(here, here, (dq, 0, 0)) for dq in range(1, n_q)]

    own_rows = pl.ds(aligned(q * per, per), per)

    def rows_of(dq):
        return pl.ds(aligned(lax.rem(q + dq, n_q) * per, per), per)

    enc_sends = [
        send(staged.at[rows_of(dq)], routed.at[own_rows], (dq, 0, 0)) for dq in range(1, n_q)
    ]
    routed[own_rows, :] = staged[own_rows, :]

    grad_load.wait()
    low_load.wait()
    low[...] = times_t(x[pl.ds(0, slots), :], w[up_rows[0], :])
    low_sends = [send(low, low_in.at[dm - 1], (0, 0, dm)) for dm in range(1, n_m)]
    down_load.wait()
    gain_load.wait()
    x[pl.ds(slots, rank), :] = (gain[...] * down[...].astype(F32)).astype(BF16)
    pass_on(0, 0)
    for j in range(n_m):
        proj_loads[j].wait()
        part[j] = times_t(x[...], w[pl.ds(j * columns, columns), :])
    part_sends = [
        send(part.at[lax.rem(m + dm, n_m)], part_in.at[dm - 1], (0, 0, dm)) for dm in range(1, n_m)
    ]
    for h in range(1, pieces):
        pass_on(0, h)
    pick_t[...] = jnp.transpose(pick).astype(BF16)

    for copy in low_sends + part_sends:
        copy.wait_recv()
    u_own = low[...]
    sums = part[m]
    for dm in range(1, n_m):
        u_own += low_in[dm - 1]
        sums += part_in[dm - 1]
    u_own = u_own.astype(BF16)
    q_own[...] = sums[slots:]
    home[...] = (sums[:slots] + times(u_own, sums[slots:].astype(BF16))).astype(BF16)
    for tick in range(1, TICKS):
        for h in range(pieces):
            pass_on(tick, h)
    home_sends = [
        send(home.at[rows_of(dq)], home_in.at[own_rows], (dq, -TICKS, 0)) for dq in range(n_q)
    ]
    q_send = send(q_own, q_in, (0, -1, 0))

    for copy in enc_sends:
        copy.wait_recv()
    stores = []
    tile = min(512, features)
    for start in range(0, features, tile):
        at = pl.ds(start, tile)
        soft[:, at] = times(routed[...], w[pl.ds(0, width), at]).astype(BF16)
        stores.append(store(soft.at[:, at], soft_hbm.at[0, :, at]))

    def layer_products(tick):
        for copy in spread[tick]:
            copy.wait_recv()
        late[tick] = times_t(x[...], w[up_rows[tick + 1], :])
        late_sends = [send(late.at[tick], late_in.at[tick, dm - 1], (0, 0, dm)) for dm in range(1, n_m)]
        for copy in late_sends:
            copy.wait_recv()
        sums = late[tick]
        for dm in range(1, n_m):
            sums += late_in[tick, dm - 1]
        tail[tick] = (sums[:slots] + times(u_own, sums[slots:].astype(BF16))).astype(BF16)
        tail_sends = [
            send(tail.at[tick, rows_of(dq)], tail_in.at[tick, own_rows], (dq, -TICKS, 0))
            for dq in range(n_q)
        ]
        return tail_sends, sums[slots:]

    tail_sends, low_mix = layer_products(0)
    m_own[...] = low_mix
    m_send = send(m_own, m_in, (0, -1, 0))
    last_sends, _ = layer_products(1)

    for copy in home_sends + [q_send, m_send] + tail_sends:
        copy.wait_recv()
    own_low = q_own[...].astype(BF16)
    mix = (q_in[...] + times(m_in[...].astype(BF16), own_low)).astype(BF16)
    behind = times(pick_t[...], tail_in[0]).astype(BF16)
    out[...] = times(pick_t[...], home_in[...]) + times(behind, mix)
    for copy in last_sends:
        copy.wait_recv()
    out[...] += times(times(pick_t[...], tail_in[1]).astype(BF16), own_low)
    stores.append(store(out, out_hbm.at[0]))
    for copy in sent:
        copy.wait_send()
    for copy in stores:
        copy.wait()


def on_device(enc_rows, proj_weight, row_owner, grad_in, adapter_gain, adapter_down, adapter_up):
    counts = tuple(lax.axis_size(axis) for axis in ("seq", "section", "mp"))
    n_q, n_z, n_m = counts
    _, slots, width = enc_rows.shape
    _, rank, features = adapter_down.shape
    columns = width // n_m
    tiles = features // min(512, features)
    pieces = 2 if features // n_q % 256 == 0 else 1
    messages = TICKS * pieces * n_q + (n_q - 1) + (2 + TICKS) * (n_m - 1) + (1 + TICKS) * n_q + 2
    flops = 2 * slots * features * (2 * width + 3 * rank)
    vmem = pltpu.VMEM
    return pl.pallas_call(
        functools.partial(kernel, counts, pieces),
        out_shape=(
            jax.ShapeDtypeStruct((1, slots, features), BF16),
            jax.ShapeDtypeStruct((1, slots, columns), F32),
        ),
        in_specs=[pl.BlockSpec(memory_space=pl.ANY)] * 7,
        out_specs=(pl.BlockSpec(memory_space=pl.ANY),) * 2,
        scratch_shapes=[
            vmem((slots, width), BF16),
            vmem((1, slots), jnp.int32),
            vmem((1, features), F32),
            vmem((rank, features), BF16),
            vmem((slots + rank, features), BF16),
            vmem((width + (TICKS + 1) * rank, features), BF16),
            vmem((slots, width), BF16),
            vmem((slots, width), BF16),
            vmem((slots, slots), BF16),
            vmem((slots, features), BF16),
            vmem((n_m, slots + rank, columns), F32),
            vmem((n_m - 1, slots + rank, columns), F32),
            vmem((slots, rank), F32),
            vmem((n_m - 1, slots, rank), F32),
            vmem((TICKS, slots + rank, rank), F32),
            vmem((TICKS, n_m - 1, slots + rank, rank), F32),
            vmem((slots, columns), BF16),
            vmem((slots, columns), BF16),
            vmem((TICKS, slots, rank), BF16),
            vmem((TICKS, slots, rank), BF16),
            vmem((rank, columns), F32),
            vmem((rank, columns), F32),
            vmem((rank, rank), F32),
            vmem((rank, rank), F32),
            vmem((slots, columns), F32),
            pltpu.SemaphoreType.DMA((6 + n_m,)),
            pltpu.SemaphoreType.DMA((tiles + 1,)),
            pltpu.SemaphoreType.DMA((messages,)),
            pltpu.SemaphoreType.DMA((messages,)),
        ],
        compiler_params=pltpu.CompilerParams(
            collective_id=0, has_side_effects=True, vmem_limit_bytes=63 * 1024 * 1024
        ),
        cost_estimate=pl.CostEstimate(flops=flops, bytes_accessed=12 * 1024 * 1024, transcendentals=0),
    )(enc_rows, proj_weight, row_owner, grad_in, adapter_gain, adapter_down, adapter_up)


def solution(mesh):
    placed = (
        P("section", "seq", None),
        P(None, "mp"),
        P("section", "seq"),
        P("section", "seq", "mp"),
        P("section", "mp"),
        P("section", None, "mp"),
        P("section", None, "mp"),
    )
    return jax.shard_map(
        on_device,
        mesh=mesh,
        in_specs=placed,
        out_specs=(P("section", "seq", "mp"), P("section", "seq", "mp")),
        check_vma=False,
    )
```

```python
import functools

import jax
import jax.numpy as jnp
from jax import lax
from jax.experimental import pallas as pl
from jax.experimental.pallas import tpu as pltpu
from jax.sharding import PartitionSpec as P

TICKS = 2
MESH = pl.DeviceIdType.MESH
F32, BF16 = jnp.float32, jnp.bfloat16


def times(a, b):
    return jnp.dot(a, b, preferred_element_type=F32)


def times_t(a, b):
    return lax.dot_general(a, b, (((1,), (1,)), ((), ())), preferred_element_type=F32)


def aligned(value, unit):
    return pl.multiple_of(value, unit)


def kernel(
    counts, pieces,
    enc_hbm, proj_hbm, owner_hbm, grad_hbm, gain_hbm, down_hbm, up_hbm,
    routed_hbm, out_hbm,
    enc, owner, gain, down, x, w, staged, routed, pick_t,
    part, part_in, low, low_in, late, late_in,
    home, home_in, tail, tail_in, q_own, q_in, m_own, m_in, out,
    load_sem, store_sem, send_sem, recv_sem,
):
    n_q, n_z, n_m = counts
    q, z, m = lax.axis_index("seq"), lax.axis_index("section"), lax.axis_index("mp")
    slots, width = enc.shape
    rank, features = down.shape
    columns = width // n_m
    per = slots // n_q
    share = features // n_q

    def device(dq, dz, dm):
        return (lax.rem(q + dq % n_q, n_q), lax.rem(z + dz % n_z, n_z), lax.rem(m + dm % n_m, n_m))

    used = [0, 0, 0]
    sent = []

    def load(src, dst):
        copy = pltpu.make_async_copy(src, dst, load_sem.at[used[0]])
        used[0] += 1
        copy.start()
        return copy

    def store(src, dst):
        copy = pltpu.make_async_copy(src, dst, store_sem.at[used[1]])
        used[1] += 1
        copy.start()
        return copy

    def send(src, dst, offsets):
        copy = pltpu.make_async_remote_copy(
            src_ref=src, dst_ref=dst,
            send_sem=send_sem.at[used[2]], recv_sem=recv_sem.at[used[2]],
            device_id=device(*offsets), device_id_type=MESH,
        )
        used[2] += 1
        copy.start()
        sent.append(copy)
        return copy

    owner_load = load(owner_hbm, owner)
    enc_load = load(enc_hbm.at[0], enc)
    low_load = load(up_hbm.at[0], w.at[pl.ds(width, rank)])
    grad_load = load(grad_hbm.at[0], x.at[pl.ds(0, slots)])
    gain_load = load(gain_hbm, gain)
    down_load = load(down_hbm.at[0], down)
    proj_loads = [
        load(proj_hbm.at[pl.ds(j * columns, columns)], w.at[pl.ds(j * columns, columns)])
        for j in range(n_m)
    ]

    targets = {(dq, 0, 0) for dq in range(1, n_q)}
    targets |= {(0, 1, 0), (0, -1 % n_z, 0)}
    targets |= {(dq, -TICKS % n_z, 0) for dq in range(n_q)}
    targets |= {(0, 0, dm) for dm in range(1, n_m)}
    barrier = pltpu.get_barrier_semaphore()
    for dq, dz, dm in sorted(targets):
        pl.semaphore_signal(barrier, inc=1, device_id=device(-dq, -dz, -dm), device_id_type=MESH)

    owner_load.wait()
    owners = owner[...].astype(F32)
    readers = lax.broadcasted_iota(jnp.int32, (max(8, n_q), slots), 0).astype(F32)
    matches = jnp.where(owners == readers, 1.0, 0.0)
    row_at = lax.broadcasted_iota(jnp.int32, (slots, slots), 0)
    column_at = lax.broadcasted_iota(jnp.int32, (slots, slots), 1)
    earlier = jnp.where(row_at < column_at, 1.0, 0.0).astype(BF16)
    before = times(matches.astype(BF16), earlier)
    order_rank = jnp.sum(matches * before, axis=0, keepdims=True)
    target = jnp.where(owners >= 0.0, owners * per + order_rank, -1.0)
    pick = jnp.where(row_at.astype(F32) == target, 1.0, 0.0)
    enc_load.wait()
    staged[...] = times(pick.astype(BF16), enc[...]).astype(BF16)
    pl.semaphore_wait(barrier, len(targets))

    piece = share // pieces
    up_rows = [pl.ds(width + tick * rank, rank) for tick in range(TICKS + 1)]

    def piece_at(h):
        return pl.ds(aligned(q * share + h * piece, 128), piece)

    ring = [
        [
            send(up_hbm.at[0, :, piece_at(h)], w.at[up_rows[1], piece_at(h)], (0, 1, 0))
            for h in range(pieces)
        ]
    ] + [[] for _ in range(1, TICKS)]
    spread = [[] for _ in range(TICKS)]

    def pass_on(tick, h):
        ring[tick][h].wait_recv()
        here = w.at[up_rows[tick + 1], piece_at(h)]
        if tick + 1 < TICKS:
            ring[tick + 1].append(send(here, w.at[up_rows[tick + 2], piece_at(h)], (0, 1, 0)))
        spread[tick] += [send(here, here, (dq, 0, 0)) for dq in range(1, n_q)]

    own_rows = pl.ds(aligned(q * per, per), per)

    def rows_of(dq):
        return pl.ds(aligned(lax.rem(q + dq, n_q) * per, per), per)

    enc_sends = [
        send(staged.at[rows_of(dq)], routed.at[own_rows], (dq, 0, 0)) for dq in range(1, n_q)
    ]
    routed[own_rows, :] = staged[own_rows, :]

    grad_load.wait()
    low_load.wait()
    low[...] = times_t(x[pl.ds(0, slots), :], w[up_rows[0], :])
    low_sends = [send(low, low_in.at[dm - 1], (0, 0, dm)) for dm in range(1, n_m)]
    down_load.wait()
    gain_load.wait()
    x[pl.ds(slots, rank), :] = (gain[...] * down[...].astype(F32)).astype(BF16)
    for h in range(pieces):
        pass_on(0, h)
    split = (n_m + 1) // 2
    for j in range(n_m):
        if j == split:
            for h in range(pieces):
                pass_on(1, h)
        proj_loads[j].wait()
        part[j] = times_t(x[...], w[pl.ds(j * columns, columns), :])
    part_sends = [
        send(part.at[lax.rem(m + dm, n_m)], part_in.at[dm - 1], (0, 0, dm)) for dm in range(1, n_m)
    ]
    pick_t[...] = jnp.transpose(pick).astype(BF16)

    for copy in low_sends + part_sends:
        copy.wait_recv()
    u_own = low[...]
    sums = part[m]
    for dm in range(1, n_m):
        u_own += low_in[dm - 1]
        sums += part_in[dm - 1]
    u_own = u_own.astype(BF16)
    q_own[...] = sums[slots:]
    home[...] = (sums[:slots] + times(u_own, sums[slots:].astype(BF16))).astype(BF16)
    home_sends = [
        send(home.at[rows_of(dq)], home_in.at[own_rows], (dq, -TICKS, 0)) for dq in range(n_q)
    ]
    q_send = send(q_own, q_in, (0, -1, 0))

    for copy in enc_sends:
        copy.wait_recv()
    stores = [store(routed, routed_hbm)]

    def share_of(dq):
        return pl.ds(aligned(lax.rem(q + dq, n_q) * share, share), share)

    def layer_products(tick):
        rows = up_rows[tick + 1]
        at = share_of(0)
        total = times_t(x[:, at], w[rows, at])
        for dq in range(1, n_q):
            for h in range(pieces):
                spread[tick][h * (n_q - 1) + dq - 1].wait_recv()
            at = share_of(n_q - dq)
            total += times_t(x[:, at], w[rows, at])
        late[tick] = total
        late_sends = [send(late.at[tick], late_in.at[tick, dm - 1], (0, 0, dm)) for dm in range(1, n_m)]
        for copy in late_sends:
            copy.wait_recv()
        sums = late[tick]
        for dm in range(1, n_m):
            sums += late_in[tick, dm - 1]
        tail[tick] = (sums[:slots] + times(u_own, sums[slots:].astype(BF16))).astype(BF16)
        tail_sends = [
            send(tail.at[tick, rows_of(dq)], tail_in.at[tick, own_rows], (dq, -TICKS, 0))
            for dq in range(n_q)
        ]
        return tail_sends, sums[slots:]

    tail_sends, low_mix = layer_products(0)
    m_own[...] = low_mix
    m_send = send(m_own, m_in, (0, -1, 0))
    last_sends, _ = layer_products(1)

    for copy in home_sends + [q_send, m_send] + tail_sends:
        copy.wait_recv()
    own_low = q_own[...].astype(BF16)
    mix = (q_in[...] + times(m_in[...].astype(BF16), own_low)).astype(BF16)
    behind = times(pick_t[...], tail_in[0]).astype(BF16)
    out[...] = times(pick_t[...], home_in[...]) + times(behind, mix)
    for copy in last_sends:
        copy.wait_recv()
    out[...] += times(times(pick_t[...], tail_in[1]).astype(BF16), own_low)
    stores.append(store(out, out_hbm.at[0]))
    for copy in sent:
        copy.wait_send()
    for copy in stores:
        copy.wait()


def on_device(enc_rows, proj_weight, row_owner, grad_in, adapter_gain, adapter_down, adapter_up):
    counts = tuple(lax.axis_size(axis) for axis in ("seq", "section", "mp"))
    n_q, n_z, n_m = counts
    _, slots, width = enc_rows.shape
    _, rank, features = adapter_down.shape
    columns = width // n_m
    pieces = 2 if features // n_q % 256 == 0 else 1
    messages = TICKS * pieces * n_q + (n_q - 1) + (2 + TICKS) * (n_m - 1) + (1 + TICKS) * n_q + 2
    flops = 2 * slots * features * (width + 3 * rank)
    vmem = pltpu.VMEM
    routed, enc_grad = pl.pallas_call(
        functools.partial(kernel, counts, pieces),
        out_shape=(
            jax.ShapeDtypeStruct((slots, width), BF16),
            jax.ShapeDtypeStruct((1, slots, columns), F32),
        ),
        in_specs=[pl.BlockSpec(memory_space=pl.ANY)] * 7,
        out_specs=(pl.BlockSpec(memory_space=pl.ANY),) * 2,
        scratch_shapes=[
            vmem((slots, width), BF16),
            vmem((1, slots), jnp.int32),
            vmem((1, features), F32),
            vmem((rank, features), BF16),
            vmem((slots + rank, features), BF16),
            vmem((width + (TICKS + 1) * rank, features), BF16),
            vmem((slots, width), BF16),
            vmem((slots, width), BF16),
            vmem((slots, slots), BF16),
            vmem((n_m, slots + rank, columns), F32),
            vmem((n_m - 1, slots + rank, columns), F32),
            vmem((slots, rank), F32),
            vmem((n_m - 1, slots, rank), F32),
            vmem((TICKS, slots + rank, rank), F32),
            vmem((TICKS, n_m - 1, slots + rank, rank), F32),
            vmem((slots, columns), BF16),
            vmem((slots, columns), BF16),
            vmem((TICKS, slots, rank), BF16),
            vmem((TICKS, slots, rank), BF16),
            vmem((rank, columns), F32),
            vmem((rank, columns), F32),
            vmem((rank, rank), F32),
            vmem((rank, rank), F32),
            vmem((slots, columns), F32),
            pltpu.SemaphoreType.DMA((6 + n_m,)),
            pltpu.SemaphoreType.DMA((2,)),
            pltpu.SemaphoreType.DMA((messages,)),
            pltpu.SemaphoreType.DMA((messages,)),
        ],
        compiler_params=pltpu.CompilerParams(
            collective_id=0, has_side_effects=True, vmem_limit_bytes=63 * 1024 * 1024
        ),
        cost_estimate=pl.CostEstimate(flops=flops, bytes_accessed=12 * 1024 * 1024, transcendentals=0),
    )(enc_rows, proj_weight, row_owner, grad_in, adapter_gain, adapter_down, adapter_up)
    return times(routed, proj_weight).astype(BF16)[None], enc_grad


def solution(mesh):
    placed = (
        P("section", "seq", None),
        P(None, "mp"),
        P("section", "seq"),
        P("section", "seq", "mp"),
        P("section", "mp"),
        P("section", None, "mp"),
        P("section", None, "mp"),
    )
    return jax.shard_map(
        on_device,
        mesh=mesh,
        in_specs=placed,
        out_specs=(P("section", "seq", "mp"), P("section", "seq", "mp")),
        check_vma=False,
    )
```

```python
import functools

import jax
import jax.numpy as jnp
from jax import lax
from jax.experimental import pallas as pl
from jax.experimental.pallas import tpu as pltpu
from jax.sharding import PartitionSpec as P

TICKS = 2
MESH = pl.DeviceIdType.MESH
F32, BF16 = jnp.float32, jnp.bfloat16


def times(a, b):
    return jnp.dot(a, b, preferred_element_type=F32)


def times_t(a, b):
    return lax.dot_general(a, b, (((1,), (1,)), ((), ())), preferred_element_type=F32)


def aligned(value, unit):
    return pl.multiple_of(value, unit)


def kernel(
    counts, pieces,
    enc_hbm, proj_hbm, owner_hbm, grad_hbm, gain_hbm, down_hbm, up_hbm,
    soft_hbm, out_hbm,
    enc, owner, gain, down, x, w, staged, routed, pick_t, soft,
    part, part_in, low, low_in, late, late_in,
    home, home_in, tail, tail_in, q_own, q_in, m_own, m_in, out,
    load_sem, store_sem, send_sem, recv_sem,
):
    n_q, n_z, n_m = counts
    q, z, m = lax.axis_index("seq"), lax.axis_index("section"), lax.axis_index("mp")
    slots, width = enc.shape
    rank, features = down.shape
    columns = width // n_m
    per = slots // n_q
    share = features // n_q

    def device(dq, dz, dm):
        return (lax.rem(q + dq % n_q, n_q), lax.rem(z + dz % n_z, n_z), lax.rem(m + dm % n_m, n_m))

    used = [0, 0, 0]
    sent = []

    def load(src, dst):
        copy = pltpu.make_async_copy(src, dst, load_sem.at[used[0]])
        used[0] += 1
        copy.start()
        return copy

    def store(src, dst):
        copy = pltpu.make_async_copy(src, dst, store_sem.at[used[1]])
        used[1] += 1
        copy.start()
        return copy

    def send(src, dst, offsets):
        copy = pltpu.make_async_remote_copy(
            src_ref=src, dst_ref=dst,
            send_sem=send_sem.at[used[2]], recv_sem=recv_sem.at[used[2]],
            device_id=device(*offsets), device_id_type=MESH,
        )
        used[2] += 1
        copy.start()
        sent.append(copy)
        return copy

    owner_load = load(owner_hbm, owner)
    enc_load = load(enc_hbm.at[0], enc)
    low_load = load(up_hbm.at[0], w.at[pl.ds(width, rank)])
    grad_load = load(grad_hbm.at[0], x.at[pl.ds(0, slots)])
    gain_load = load(gain_hbm, gain)
    down_load = load(down_hbm.at[0], down)
    proj_loads = [
        load(proj_hbm.at[pl.ds(j * columns, columns)], w.at[pl.ds(j * columns, columns)])
        for j in range(n_m)
    ]

    targets = {(dq, 0, 0) for dq in range(1, n_q)}
    targets |= {(0, 1, 0), (0, -1 % n_z, 0)}
    targets |= {(dq, -TICKS % n_z, 0) for dq in range(n_q)}
    targets |= {(0, 0, dm) for dm in range(1, n_m)}
    barrier = pltpu.get_barrier_semaphore()
    for dq, dz, dm in sorted(targets):
        pl.semaphore_signal(barrier, inc=1, device_id=device(-dq, -dz, -dm), device_id_type=MESH)

    pl.semaphore_wait(barrier, len(targets))

    piece = share // pieces
    up_rows = [pl.ds(width + tick * rank, rank) for tick in range(TICKS + 1)]

    def piece_at(h):
        return pl.ds(aligned(q * share + h * piece, 128), piece)

    ring = [
        [
            send(up_hbm.at[0, :, piece_at(h)], w.at[up_rows[1], piece_at(h)], (0, 1, 0))
            for h in range(pieces)
        ]
    ] + [[] for _ in range(1, TICKS)]
    spread = [[] for _ in range(TICKS)]

    def pass_on(tick, h):
        ring[tick][h].wait_recv()
        here = w.at[up_rows[tick + 1], piece_at(h)]
        if tick + 1 < TICKS:
            ring[tick + 1].append(send(here, w.at[up_rows[tick + 2], piece_at(h)], (0, 1, 0)))
        spread[tick] += [send(here, here, (dq, 0, 0)) for dq in range(1, n_q)]

    owner_load.wait()
    owners = owner[...].astype(F32)
    readers = lax.broadcasted_iota(jnp.int32, (max(8, n_q), slots), 0).astype(F32)
    matches = jnp.where(owners == readers, 1.0, 0.0)
    row_at = lax.broadcasted_iota(jnp.int32, (slots, slots), 0)
    column_at = lax.broadcasted_iota(jnp.int32, (slots, slots), 1)
    earlier = jnp.where(row_at < column_at, 1.0, 0.0).astype(BF16)
    before = times(matches.astype(BF16), earlier)
    order_rank = jnp.sum(matches * before, axis=0, keepdims=True)
    target = jnp.where(owners >= 0.0, owners * per + order_rank, -1.0)
    pick = jnp.where(row_at.astype(F32) == target, 1.0, 0.0)
    enc_load.wait()
    staged[...] = times(pick.astype(BF16), enc[...]).astype(BF16)
    own_rows = pl.ds(aligned(q * per, per), per)

    def rows_of(dq):
        return pl.ds(aligned(lax.rem(q + dq, n_q) * per, per), per)

    enc_sends = [
        send(staged.at[rows_of(dq)], routed.at[own_rows], (dq, 0, 0)) for dq in range(1, n_q)
    ]
    routed[own_rows, :] = staged[own_rows, :]

    for h in range(pieces):
        pass_on(0, h)
    pick_t[...] = jnp.transpose(pick).astype(BF16)

    grad_load.wait()
    low_load.wait()
    low[...] = times_t(x[pl.ds(0, slots), :], w[up_rows[0], :])
    low_sends = [send(low, low_in.at[dm - 1], (0, 0, dm)) for dm in range(1, n_m)]
    down_load.wait()
    gain_load.wait()
    x[pl.ds(slots, rank), :] = (gain[...] * down[...].astype(F32)).astype(BF16)
    for tick in range(1, TICKS):
        for h in range(pieces):
            pass_on(tick, h)
    for copy in proj_loads:
        copy.wait()
    part_sends = []
    for dm in [*range(1, n_m), 0]:
        block = pl.ds(aligned(lax.rem(m + dm, n_m) * columns, columns), columns)
        part[dm] = times_t(x[...], w[block, :])
        if dm:
            part_sends.append(send(part.at[dm], part_in.at[dm - 1], (0, 0, dm)))

    def share_of(dq):
        return pl.ds(aligned(lax.rem(q + dq, n_q) * share, share), share)

    def late_products(tick):
        rows = up_rows[tick + 1]
        at = share_of(0)
        total = times_t(x[:, at], w[rows, at])
        for dq in range(1, n_q):
            for h in range(pieces):
                spread[tick][h * (n_q - 1) + dq - 1].wait_recv()
            at = share_of(n_q - dq)
            total += times_t(x[:, at], w[rows, at])
        late[tick] = total
        return [send(late.at[tick], late_in.at[tick, dm - 1], (0, 0, dm)) for dm in range(1, n_m)]

    def late_rows(tick, late_sends):
        for copy in late_sends:
            copy.wait_recv()
        sums = late[tick]
        for dm in range(1, n_m):
            sums += late_in[tick, dm - 1]
        tail[tick] = (sums[:slots] + times(u_own, sums[slots:].astype(BF16))).astype(BF16)
        tail_sends = [
            send(tail.at[tick, rows_of(dq)], tail_in.at[tick, own_rows], (dq, -TICKS, 0))
            for dq in range(n_q)
        ]
        return tail_sends, sums[slots:]

    late_sends = late_products(0)
    for copy in low_sends + part_sends:
        copy.wait_recv()
    u_own = low[...]
    sums = part[0]
    for dm in range(1, n_m):
        u_own += low_in[dm - 1]
        sums += part_in[dm - 1]
    u_own = u_own.astype(BF16)
    q_own[...] = sums[slots:]
    q_send = send(q_own, q_in, (0, -1, 0))
    home[...] = (sums[:slots] + times(u_own, sums[slots:].astype(BF16))).astype(BF16)
    home_sends = [
        send(home.at[rows_of(dq)], home_in.at[own_rows], (dq, -TICKS, 0)) for dq in range(n_q)
    ]
    tail_sends, low_mix = late_rows(0, late_sends)
    m_own[...] = low_mix
    m_send = send(m_own, m_in, (0, -1, 0))

    for copy in enc_sends:
        copy.wait_recv()
    stores = []
    tile = min(512, features)

    def soft_tokens(tiles):
        for t in tiles:
            at = pl.ds(t * tile, tile)
            soft[:, at] = times(routed[...], w[pl.ds(0, width), at]).astype(BF16)
            stores.append(store(soft.at[:, at], soft_hbm.at[0, :, at]))

    n_tiles = features // tile
    late_sends = late_products(1)
    soft_tokens(range(n_tiles // 4))
    last_sends, _ = late_rows(1, late_sends)
    soft_tokens(range(n_tiles // 4, n_tiles))

    for copy in home_sends + [q_send, m_send] + tail_sends:
        copy.wait_recv()
    own_low = q_own[...].astype(BF16)
    mix = (q_in[...] + times(m_in[...].astype(BF16), own_low)).astype(BF16)
    behind = times(pick_t[...], tail_in[0]).astype(BF16)
    out[...] = times(pick_t[...], home_in[...]) + times(behind, mix)
    for copy in last_sends:
        copy.wait_recv()
    out[...] += times(times(pick_t[...], tail_in[1]).astype(BF16), own_low)
    stores.append(store(out, out_hbm.at[0]))
    for copy in sent:
        copy.wait_send()
    for copy in stores:
        copy.wait()


def hand_on(soft_from, out_from, soft_to, out_to, sems):
    slots = soft_from.shape[1]
    bands = sems.shape[0] - 1
    band = slots // bands
    copies = [pltpu.make_async_copy(out_from, out_to, sems.at[bands])]
    for i in range(bands):
        at = pl.ds(i * band, band)
        copies.append(pltpu.make_async_copy(soft_from.at[:, at], soft_to.at[:, at], sems.at[i]))
    for copy in copies:
        copy.start()
    for copy in copies:
        copy.wait()


def on_device(enc_rows, proj_weight, row_owner, grad_in, adapter_gain, adapter_down, adapter_up):
    counts = tuple(lax.axis_size(axis) for axis in ("seq", "section", "mp"))
    n_q, n_z, n_m = counts
    _, slots, width = enc_rows.shape
    _, rank, features = adapter_down.shape
    columns = width // n_m
    pieces = 2 if features // n_q % 256 == 0 else 1
    messages = TICKS * pieces * n_q + (n_q - 1) + (2 + TICKS) * (n_m - 1) + (1 + TICKS) * n_q + 2
    flops = 2 * slots * features * (width + 3 * rank)
    vmem = pltpu.VMEM
    results = (
        jax.ShapeDtypeStruct((1, slots, features), BF16),
        jax.ShapeDtypeStruct((1, slots, columns), F32),
    )
    soft, enc_grad = pl.pallas_call(
        functools.partial(kernel, counts, pieces),
        out_shape=results,
        in_specs=[pl.BlockSpec(memory_space=pl.ANY)] * 7,
        out_specs=(pl.BlockSpec(memory_space=pl.ANY),) * 2,
        scratch_shapes=[
            vmem((slots, width), BF16),
            vmem((1, slots), jnp.int32),
            vmem((1, features), F32),
            vmem((rank, features), BF16),
            vmem((slots + rank, features), BF16),
            vmem((width + (TICKS + 1) * rank, features), BF16),
            vmem((slots, width), BF16),
            vmem((slots, width), BF16),
            vmem((slots, slots), BF16),
            vmem((slots, features), BF16),
            vmem((n_m, slots + rank, columns), F32),
            vmem((n_m - 1, slots + rank, columns), F32),
            vmem((slots, rank), F32),
            vmem((n_m - 1, slots, rank), F32),
            vmem((TICKS, slots + rank, rank), F32),
            vmem((TICKS, n_m - 1, slots + rank, rank), F32),
            vmem((slots, columns), BF16),
            vmem((slots, columns), BF16),
            vmem((TICKS, slots, rank), BF16),
            vmem((TICKS, slots, rank), BF16),
            vmem((rank, columns), F32),
            vmem((rank, columns), F32),
            vmem((rank, rank), F32),
            vmem((rank, rank), F32),
            vmem((slots, columns), F32),
            pltpu.SemaphoreType.DMA((6 + n_m,)),
            pltpu.SemaphoreType.DMA((features // min(512, features) + 1,)),
            pltpu.SemaphoreType.DMA((messages,)),
            pltpu.SemaphoreType.DMA((messages,)),
        ],
        compiler_params=pltpu.CompilerParams(
            collective_id=0, has_side_effects=True, vmem_limit_bytes=63 * 1024 * 1024
        ),
        cost_estimate=pl.CostEstimate(flops=flops, bytes_accessed=12 * 1024 * 1024, transcendentals=0),
    )(enc_rows, proj_weight, row_owner, grad_in, adapter_gain, adapter_down, adapter_up)
    return pl.pallas_call(
        hand_on,
        out_shape=results,
        in_specs=[pl.BlockSpec(memory_space=pl.ANY)] * 2,
        out_specs=(pl.BlockSpec(memory_space=pl.ANY),) * 2,
        scratch_shapes=[pltpu.SemaphoreType.DMA((9,))],
        compiler_params=pltpu.CompilerParams(vmem_limit_bytes=63 * 1024 * 1024),
        cost_estimate=pl.CostEstimate(flops=0, bytes_accessed=5 * 1024 * 1024, transcendentals=0),
    )(soft, enc_grad)


def solution(mesh):
    placed = (
        P("section", "seq", None),
        P(None, "mp"),
        P("section", "seq"),
        P("section", "seq", "mp"),
        P("section", "mp"),
        P("section", None, "mp"),
        P("section", None, "mp"),
    )
    return jax.shard_map(
        on_device,
        mesh=mesh,
        in_specs=placed,
        out_specs=(P("section", "seq", "mp"), P("section", "seq", "mp")),
        check_vma=False,
    )
```

```python
import functools

import jax
import jax.numpy as jnp
from jax import lax
from jax.experimental import pallas as pl
from jax.experimental.pallas import tpu as pltpu
from jax.sharding import PartitionSpec as P

TICKS = 2
MESH = pl.DeviceIdType.MESH
F32, BF16 = jnp.float32, jnp.bfloat16


def times(a, b):
    return jnp.dot(a, b, preferred_element_type=F32)


def times_t(a, b):
    return lax.dot_general(a, b, (((1,), (1,)), ((), ())), preferred_element_type=F32)


def aligned(value, unit):
    return pl.multiple_of(value, unit)


def kernel(
    counts, pieces,
    enc_hbm, proj_hbm, owner_hbm, grad_hbm, gain_hbm, down_hbm, up_hbm,
    soft_hbm, out_hbm,
    enc, owner, gain, down, x, w, staged, routed, pick_t, soft,
    part, part_in, low, low_in, late, late_in,
    home, home_in, tail, tail_in, q_own, q_in, m_own, m_in, out,
    load_sem, store_sem, send_sem, recv_sem,
):
    n_q, n_z, n_m = counts
    q, z, m = lax.axis_index("seq"), lax.axis_index("section"), lax.axis_index("mp")
    slots, width = enc.shape
    rank, features = down.shape
    columns = width // n_m
    per = slots // n_q
    share = features // n_q

    def device(dq, dz, dm):
        return (lax.rem(q + dq % n_q, n_q), lax.rem(z + dz % n_z, n_z), lax.rem(m + dm % n_m, n_m))

    used = [0, 0, 0]
    sent = []

    def load(src, dst):
        copy = pltpu.make_async_copy(src, dst, load_sem.at[used[0]])
        used[0] += 1
        copy.start()
        return copy

    def store(src, dst):
        copy = pltpu.make_async_copy(src, dst, store_sem.at[used[1]])
        used[1] += 1
        copy.start()
        return copy

    def send(src, dst, offsets):
        copy = pltpu.make_async_remote_copy(
            src_ref=src, dst_ref=dst,
            send_sem=send_sem.at[used[2]], recv_sem=recv_sem.at[used[2]],
            device_id=device(*offsets), device_id_type=MESH,
        )
        used[2] += 1
        copy.start()
        sent.append(copy)
        return copy

    owner_load = load(owner_hbm, owner)
    enc_load = load(enc_hbm.at[0], enc)
    low_load = load(up_hbm.at[0], w.at[pl.ds(width, rank)])
    grad_load = load(grad_hbm.at[0], x.at[pl.ds(0, slots)])
    gain_load = load(gain_hbm, gain)
    down_load = load(down_hbm.at[0], down)
    proj_loads = [
        load(proj_hbm.at[pl.ds(j * columns, columns)], w.at[pl.ds(j * columns, columns)])
        for j in range(n_m)
    ]

    targets = {(dq, 0, 0) for dq in range(1, n_q)}
    targets |= {(0, dz % n_z, 0) for dz in [-1, *range(1, TICKS + 1)]}
    targets |= {(dq, -TICKS % n_z, 0) for dq in range(n_q)}
    targets |= {(0, 0, dm) for dm in range(1, n_m)}
    barrier = pltpu.get_barrier_semaphore()
    for dq, dz, dm in sorted(targets):
        pl.semaphore_signal(barrier, inc=1, device_id=device(-dq, -dz, -dm), device_id_type=MESH)

    pl.semaphore_wait(barrier, len(targets))

    piece = share // pieces
    up_rows = [pl.ds(width + tick * rank, rank) for tick in range(TICKS + 1)]

    def piece_at(h):
        return pl.ds(aligned(q * share + h * piece, 128), piece)

    low_load.wait()
    ring = [
        [
            send(w.at[up_rows[0], piece_at(h)], w.at[up_rows[tick], piece_at(h)], (0, tick, 0))
            for h in range(pieces)
        ]
        for tick in range(1, TICKS + 1)
    ]
    spread = [[] for _ in range(TICKS)]

    def pass_on(tick, h):
        ring[tick][h].wait_recv()
        here = w.at[up_rows[tick + 1], piece_at(h)]
        spread[tick] += [send(here, here, (dq, 0, 0)) for dq in range(1, n_q)]

    owner_load.wait()
    owners = owner[...].astype(F32)
    readers = lax.broadcasted_iota(jnp.int32, (max(8, n_q), slots), 0).astype(F32)
    matches = jnp.where(owners == readers, 1.0, 0.0)
    row_at = lax.broadcasted_iota(jnp.int32, (slots, slots), 0)
    column_at = lax.broadcasted_iota(jnp.int32, (slots, slots), 1)
    earlier = jnp.where(row_at < column_at, 1.0, 0.0).astype(BF16)
    before = times(matches.astype(BF16), earlier)
    order_rank = jnp.sum(matches * before, axis=0, keepdims=True)
    target = jnp.where(owners >= 0.0, owners * per + order_rank, -1.0)
    pick = jnp.where(row_at.astype(F32) == target, 1.0, 0.0)
    enc_load.wait()
    staged[...] = times(pick.astype(BF16), enc[...]).astype(BF16)
    own_rows = pl.ds(aligned(q * per, per), per)

    def rows_of(dq):
        return pl.ds(aligned(lax.rem(q + dq, n_q) * per, per), per)

    enc_sends = [
        send(staged.at[rows_of(dq)], routed.at[own_rows], (dq, 0, 0)) for dq in range(1, n_q)
    ]
    routed[own_rows, :] = staged[own_rows, :]

    for h in range(pieces):
        pass_on(0, h)
    pick_t[...] = jnp.transpose(pick).astype(BF16)

    grad_load.wait()
    low[...] = times_t(x[pl.ds(0, slots), :], w[up_rows[0], :])
    low_sends = [send(low, low_in.at[dm - 1], (0, 0, dm)) for dm in range(1, n_m)]
    down_load.wait()
    gain_load.wait()
    x[pl.ds(slots, rank), :] = (gain[...] * down[...].astype(F32)).astype(BF16)
    for tick in range(1, TICKS):
        for h in range(pieces):
            pass_on(tick, h)
    for copy in proj_loads:
        copy.wait()
    part_sends = []
    for dm in [*range(1, n_m), 0]:
        block = pl.ds(aligned(lax.rem(m + dm, n_m) * columns, columns), columns)
        part[dm] = times_t(x[...], w[block, :])
        if dm:
            part_sends.append(send(part.at[dm], part_in.at[dm - 1], (0, 0, dm)))

    def share_of(dq):
        return pl.ds(aligned(lax.rem(q + dq, n_q) * share, share), share)

    def late_products(tick):
        rows = up_rows[tick + 1]
        at = share_of(0)
        total = times_t(x[:, at], w[rows, at])
        for dq in range(1, n_q):
            for h in range(pieces):
                spread[tick][h * (n_q - 1) + dq - 1].wait_recv()
            at = share_of(n_q - dq)
            total += times_t(x[:, at], w[rows, at])
        late[tick] = total
        return [send(late.at[tick], late_in.at[tick, dm - 1], (0, 0, dm)) for dm in range(1, n_m)]

    def late_rows(tick, late_sends):
        for copy in late_sends:
            copy.wait_recv()
        sums = late[tick]
        for dm in range(1, n_m):
            sums += late_in[tick, dm - 1]
        tail[tick] = (sums[:slots] + times(u_own, sums[slots:].astype(BF16))).astype(BF16)
        tail_sends = [
            send(tail.at[tick, rows_of(dq)], tail_in.at[tick, own_rows], (dq, -TICKS, 0))
            for dq in range(n_q)
        ]
        return tail_sends, sums[slots:]

    late_sends = late_products(0)
    for copy in low_sends + part_sends:
        copy.wait_recv()
    u_own = low[...]
    sums = part[0]
    for dm in range(1, n_m):
        u_own += low_in[dm - 1]
        sums += part_in[dm - 1]
    u_own = u_own.astype(BF16)
    q_own[...] = sums[slots:]
    q_send = send(q_own, q_in, (0, -1, 0))
    home[...] = (sums[:slots] + times(u_own, sums[slots:].astype(BF16))).astype(BF16)
    home_sends = [
        send(home.at[rows_of(dq)], home_in.at[own_rows], (dq, -TICKS, 0)) for dq in range(n_q)
    ]
    tail_sends, low_mix = late_rows(0, late_sends)
    m_own[...] = low_mix
    m_send = send(m_own, m_in, (0, -1, 0))

    for copy in enc_sends:
        copy.wait_recv()
    stores = []
    tile = min(512, features)

    def soft_tokens(tiles):
        for t in tiles:
            at = pl.ds(t * tile, tile)
            soft[:, at] = times(routed[...], w[pl.ds(0, width), at]).astype(BF16)
            stores.append(store(soft.at[:, at], soft_hbm.at[0, :, at]))

    n_tiles = features // tile
    late_sends = late_products(1)
    soft_tokens(range(n_tiles // 4))
    last_sends, _ = late_rows(1, late_sends)
    soft_tokens(range(n_tiles // 4, n_tiles))

    for copy in home_sends + [q_send, m_send] + tail_sends:
        copy.wait_recv()
    own_low = q_own[...].astype(BF16)
    mix = (q_in[...] + times(m_in[...].astype(BF16), own_low)).astype(BF16)
    behind = times(pick_t[...], tail_in[0]).astype(BF16)
    out[...] = times(pick_t[...], home_in[...]) + times(behind, mix)
    for copy in last_sends:
        copy.wait_recv()
    out[...] += times(times(pick_t[...], tail_in[1]).astype(BF16), own_low)
    stores.append(store(out, out_hbm.at[0]))
    for copy in sent:
        copy.wait_send()
    for copy in stores:
        copy.wait()


def hand_on(soft_from, out_from, soft_to, out_to, soft, out, in_sem, out_sem):
    slots = soft.shape[0]
    bands = in_sem.shape[0] - 1
    band = slots // bands
    moves = [
        (soft_from.at[0, pl.ds(i * band, band)], soft.at[pl.ds(i * band, band)], soft_to.at[0, pl.ds(i * band, band)])
        for i in range(bands)
    ] + [(out_from.at[0], out, out_to.at[0])]
    loads = [pltpu.make_async_copy(a, b, in_sem.at[i]) for i, (a, b, _) in enumerate(moves)]
    stores = [pltpu.make_async_copy(b, c, out_sem.at[i]) for i, (_, b, c) in enumerate(moves)]
    for copy in loads:
        copy.start()
    for before, after in zip(loads, stores):
        before.wait()
        after.start()
    for copy in stores:
        copy.wait()


def on_device(enc_rows, proj_weight, row_owner, grad_in, adapter_gain, adapter_down, adapter_up):
    counts = tuple(lax.axis_size(axis) for axis in ("seq", "section", "mp"))
    n_q, n_z, n_m = counts
    _, slots, width = enc_rows.shape
    _, rank, features = adapter_down.shape
    columns = width // n_m
    pieces = 2 if features // n_q % 256 == 0 else 1
    messages = TICKS * pieces * n_q + (n_q - 1) + (2 + TICKS) * (n_m - 1) + (1 + TICKS) * n_q + 2
    flops = 2 * slots * features * (width + 3 * rank)
    vmem = pltpu.VMEM
    results = (
        jax.ShapeDtypeStruct((1, slots, features), BF16),
        jax.ShapeDtypeStruct((1, slots, columns), F32),
    )
    soft, enc_grad = pl.pallas_call(
        functools.partial(kernel, counts, pieces),
        out_shape=results,
        in_specs=[pl.BlockSpec(memory_space=pl.ANY)] * 7,
        out_specs=(pl.BlockSpec(memory_space=pl.ANY),) * 2,
        scratch_shapes=[
            vmem((slots, width), BF16),
            vmem((1, slots), jnp.int32),
            vmem((1, features), F32),
            vmem((rank, features), BF16),
            vmem((slots + rank, features), BF16),
            vmem((width + (TICKS + 1) * rank, features), BF16),
            vmem((slots, width), BF16),
            vmem((slots, width), BF16),
            vmem((slots, slots), BF16),
            vmem((slots, features), BF16),
            vmem((n_m, slots + rank, columns), F32),
            vmem((n_m - 1, slots + rank, columns), F32),
            vmem((slots, rank), F32),
            vmem((n_m - 1, slots, rank), F32),
            vmem((TICKS, slots + rank, rank), F32),
            vmem((TICKS, n_m - 1, slots + rank, rank), F32),
            vmem((slots, columns), BF16),
            vmem((slots, columns), BF16),
            vmem((TICKS, slots, rank), BF16),
            vmem((TICKS, slots, rank), BF16),
            vmem((rank, columns), F32),
            vmem((rank, columns), F32),
            vmem((rank, rank), F32),
            vmem((rank, rank), F32),
            vmem((slots, columns), F32),
            pltpu.SemaphoreType.DMA((6 + n_m,)),
            pltpu.SemaphoreType.DMA((features // min(512, features) + 1,)),
            pltpu.SemaphoreType.DMA((messages,)),
            pltpu.SemaphoreType.DMA((messages,)),
        ],
        compiler_params=pltpu.CompilerParams(
            collective_id=0, has_side_effects=True, vmem_limit_bytes=63 * 1024 * 1024
        ),
        cost_estimate=pl.CostEstimate(flops=flops, bytes_accessed=12 * 1024 * 1024, transcendentals=0),
    )(enc_rows, proj_weight, row_owner, grad_in, adapter_gain, adapter_down, adapter_up)
    return pl.pallas_call(
        hand_on,
        out_shape=results,
        in_specs=[pl.BlockSpec(memory_space=pl.ANY)] * 2,
        out_specs=(pl.BlockSpec(memory_space=pl.ANY),) * 2,
        scratch_shapes=[
            vmem((slots, features), BF16),
            vmem((slots, columns), F32),
            pltpu.SemaphoreType.DMA((9,)),
            pltpu.SemaphoreType.DMA((9,)),
        ],
        compiler_params=pltpu.CompilerParams(vmem_limit_bytes=63 * 1024 * 1024),
        cost_estimate=pl.CostEstimate(flops=0, bytes_accessed=5 * 1024 * 1024, transcendentals=0),
    )(soft, enc_grad)


def solution(mesh):
    placed = (
        P("section", "seq", None),
        P(None, "mp"),
        P("section", "seq"),
        P("section", "seq", "mp"),
        P("section", "mp"),
        P("section", None, "mp"),
        P("section", None, "mp"),
    )
    return jax.shard_map(
        on_device,
        mesh=mesh,
        in_specs=placed,
        out_specs=(P("section", "seq", "mp"), P("section", "seq", "mp")),
        check_vma=False,
    )
```

```python
import functools

import jax
import jax.numpy as jnp
from jax import lax
from jax.experimental import pallas as pl
from jax.experimental.pallas import tpu as pltpu
from jax.sharding import PartitionSpec as P

TICKS = 2
MESH = pl.DeviceIdType.MESH
F32, BF16 = jnp.float32, jnp.bfloat16


def times(a, b):
    return jnp.dot(a, b, preferred_element_type=F32)


def times_t(a, b):
    return lax.dot_general(a, b, (((1,), (1,)), ((), ())), preferred_element_type=F32)


def aligned(value, unit):
    return pl.multiple_of(value, unit)


def kernel(
    counts, pieces,
    enc_hbm, proj_hbm, owner_hbm, grad_hbm, gain_hbm, down_hbm, up_hbm,
    soft_hbm, out_hbm,
    enc, owner, gain, down, x, w, staged, routed, pick_t, soft,
    part, part_in, low, low_in, late, late_in,
    home, home_in, tail, tail_in, q_own, q_in, m_own, m_in, out,
    load_sem, store_sem, send_sem, recv_sem, line_send, line_recv, spread_send, spread_recv,
):
    n_q, n_z, n_m = counts
    q, z, m = lax.axis_index("seq"), lax.axis_index("section"), lax.axis_index("mp")
    slots, width = enc.shape
    rank, features = down.shape
    columns = width // n_m
    per = slots // n_q
    share = features // n_q

    def device(dq, dz, dm):
        return (lax.rem(q + dq % n_q, n_q), lax.rem(z + dz % n_z, n_z), lax.rem(m + dm % n_m, n_m))

    used = [0, 0, 0]
    sent = []

    def load(src, dst):
        copy = pltpu.make_async_copy(src, dst, load_sem.at[used[0]])
        used[0] += 1
        copy.start()
        return copy

    def store(src, dst):
        copy = pltpu.make_async_copy(src, dst, store_sem.at[used[1]])
        used[1] += 1
        copy.start()
        return copy

    def send(src, dst, offsets):
        copy = pltpu.make_async_remote_copy(
            src_ref=src, dst_ref=dst,
            send_sem=send_sem.at[used[2]], recv_sem=recv_sem.at[used[2]],
            device_id=device(*offsets), device_id_type=MESH,
        )
        used[2] += 1
        copy.start()
        sent.append(copy)
        return copy

    owner_load = load(owner_hbm, owner)
    enc_load = load(enc_hbm.at[0], enc)
    low_load = load(up_hbm.at[0], w.at[pl.ds(width, rank)])
    grad_load = load(grad_hbm.at[0], x.at[pl.ds(0, slots)])
    gain_load = load(gain_hbm, gain)
    down_load = load(down_hbm.at[0], down)
    proj_loads = [
        load(proj_hbm.at[pl.ds(j * columns, columns)], w.at[pl.ds(j * columns, columns)])
        for j in range(n_m)
    ]

    targets = {(dq, 0, 0) for dq in range(1, n_q)}
    targets |= {(0, dz % n_z, 0) for dz in (-1, 1)}
    targets |= {(dq, -TICKS % n_z, 0) for dq in range(n_q)}
    targets |= {(0, 0, dm) for dm in range(1, n_m)}
    barrier = pltpu.get_barrier_semaphore()
    for dq, dz, dm in sorted(targets):
        pl.semaphore_signal(barrier, inc=1, device_id=device(-dq, -dz, -dm), device_id_type=MESH)

    pl.semaphore_wait(barrier, len(targets))

    piece = share // pieces
    up_rows = [pl.ds(width + tick * rank, rank) for tick in range(TICKS + 1)]

    def piece_at(h):
        return pl.ds(aligned(q * share + h * piece, 128), piece)

    if n_z == 4 and TICKS == 2:
        plan = [(0, 1, 1, (0, 1, 2)), (0, 2, -2, (2, 3)), (1, 2, 1, (1, 2)), (2, 1, -1, (1,))]
        swapped = z == 0
    else:
        plan = [(tick, tick + 1, 1, None) for tick in range(TICKS)]
        swapped = None

    def only(sections, act):
        if sections is None:
            act()
        else:
            chosen = z == sections[0]
            for section in sections[1:]:
                chosen = jnp.logical_or(chosen, z == section)
            pl.when(chosen)(act)

    def along(entry, h):
        source, slot, dz, _ = plan[entry]
        return pltpu.make_async_remote_copy(
            src_ref=w.at[up_rows[source], piece_at(h)], dst_ref=w.at[up_rows[slot], piece_at(h)],
            send_sem=line_send.at[entry * pieces + h], recv_sem=line_recv.at[(slot - 1) * pieces + h],
            device_id=device(0, dz, 0), device_id_type=MESH,
        )

    def send_from(slot, h):
        for entry, (source, _, _, sections) in enumerate(plan):
            if source == slot:
                only(sections, along(entry, h).start)

    low_load.wait()
    for h in range(pieces):
        send_from(0, h)

    def described(tick, h, dq):
        here = w.at[up_rows[tick + 1], piece_at(h)]
        at = (tick * pieces + h) * (n_q - 1) + dq - 1
        return pltpu.make_async_remote_copy(
            src_ref=here, dst_ref=here, send_sem=spread_send.at[at], recv_sem=spread_recv.at[at],
            device_id=device(dq, 0, 0), device_id_type=MESH,
        )

    spread = [
        [described(tick, h, dq) for h in range(pieces) for dq in range(1, n_q)] for tick in range(TICKS)
    ]

    def pass_slot(tick):
        for h in range(pieces):
            along([slot for _, slot, _, _ in plan].index(tick + 1), h).wait_recv()
            send_from(tick + 1, h)
            for dq in range(1, n_q):
                spread[tick][h * (n_q - 1) + dq - 1].start()

    def pass_on(tick):
        if swapped is None:
            pass_slot(tick)
        else:
            pl.when(swapped)(lambda: pass_slot(TICKS - 1 - tick))
            pl.when(jnp.logical_not(swapped))(lambda: pass_slot(tick))

    owner_load.wait()
    owners = owner[...].astype(F32)
    readers = lax.broadcasted_iota(jnp.int32, (max(8, n_q), slots), 0).astype(F32)
    matches = jnp.where(owners == readers, 1.0, 0.0)
    row_at = lax.broadcasted_iota(jnp.int32, (slots, slots), 0)
    column_at = lax.broadcasted_iota(jnp.int32, (slots, slots), 1)
    earlier = jnp.where(row_at < column_at, 1.0, 0.0).astype(BF16)
    before = times(matches.astype(BF16), earlier)
    order_rank = jnp.sum(matches * before, axis=0, keepdims=True)
    target = jnp.where(owners >= 0.0, owners * per + order_rank, -1.0)
    pick = jnp.where(row_at.astype(F32) == target, 1.0, 0.0)
    enc_load.wait()
    staged[...] = times(pick.astype(BF16), enc[...]).astype(BF16)
    own_rows = pl.ds(aligned(q * per, per), per)

    def rows_of(dq):
        return pl.ds(aligned(lax.rem(q + dq, n_q) * per, per), per)

    enc_sends = [
        send(staged.at[rows_of(dq)], routed.at[own_rows], (dq, 0, 0)) for dq in range(1, n_q)
    ]
    routed[own_rows, :] = staged[own_rows, :]

    pass_on(0)
    pick_t[...] = jnp.transpose(pick).astype(BF16)

    grad_load.wait()
    low[...] = times_t(x[pl.ds(0, slots), :], w[up_rows[0], :])
    low_sends = [send(low, low_in.at[dm - 1], (0, 0, dm)) for dm in range(1, n_m)]
    down_load.wait()
    gain_load.wait()
    x[pl.ds(slots, rank), :] = (gain[...] * down[...].astype(F32)).astype(BF16)
    for tick in range(1, TICKS):
        pass_on(tick)
    for copy in proj_loads:
        copy.wait()
    part_sends = []
    for dm in [*range(1, n_m), 0]:
        block = pl.ds(aligned(lax.rem(m + dm, n_m) * columns, columns), columns)
        part[dm] = times_t(x[...], w[block, :])
        if dm:
            part_sends.append(send(part.at[dm], part_in.at[dm - 1], (0, 0, dm)))

    def share_of(dq):
        return pl.ds(aligned(lax.rem(q + dq, n_q) * share, share), share)

    def late_products(tick):
        rows = up_rows[tick + 1]
        at = share_of(0)
        total = times_t(x[:, at], w[rows, at])
        for dq in range(1, n_q):
            for h in range(pieces):
                spread[tick][h * (n_q - 1) + dq - 1].wait_recv()
            at = share_of(n_q - dq)
            total += times_t(x[:, at], w[rows, at])
        late[tick] = total
        return [send(late.at[tick], late_in.at[tick, dm - 1], (0, 0, dm)) for dm in range(1, n_m)]

    def late_rows(tick, late_sends):
        for copy in late_sends:
            copy.wait_recv()
        sums = late[tick]
        for dm in range(1, n_m):
            sums += late_in[tick, dm - 1]
        tail[tick] = (sums[:slots] + times(u_own, sums[slots:].astype(BF16))).astype(BF16)
        tail_sends = [
            send(tail.at[tick, rows_of(dq)], tail_in.at[tick, own_rows], (dq, -TICKS, 0))
            for dq in range(n_q)
        ]
        return tail_sends, sums[slots:]

    late_sends = late_products(0)
    for copy in low_sends + part_sends:
        copy.wait_recv()
    u_own = low[...]
    sums = part[0]
    for dm in range(1, n_m):
        u_own += low_in[dm - 1]
        sums += part_in[dm - 1]
    u_own = u_own.astype(BF16)
    q_own[...] = sums[slots:]
    q_send = send(q_own, q_in, (0, -1, 0))
    home[...] = (sums[:slots] + times(u_own, sums[slots:].astype(BF16))).astype(BF16)
    home_sends = [
        send(home.at[rows_of(dq)], home_in.at[own_rows], (dq, -TICKS, 0)) for dq in range(n_q)
    ]
    tail_sends, low_mix = late_rows(0, late_sends)
    m_own[...] = low_mix
    m_send = send(m_own, m_in, (0, -1, 0))

    for copy in enc_sends:
        copy.wait_recv()
    stores = []
    tile = min(512, features)

    def soft_tokens(tiles):
        for t in tiles:
            at = pl.ds(t * tile, tile)
            soft[:, at] = times(routed[...], w[pl.ds(0, width), at]).astype(BF16)
            stores.append(store(soft.at[:, at], soft_hbm.at[0, :, at]))

    n_tiles = features // tile
    late_sends = late_products(1)
    soft_tokens(range(n_tiles // 4))
    last_sends, _ = late_rows(1, late_sends)
    soft_tokens(range(n_tiles // 4, n_tiles))

    for copy in home_sends + [q_send, m_send] + tail_sends:
        copy.wait_recv()
    own_low = q_own[...].astype(BF16)
    mix = (q_in[...] + times(m_in[...].astype(BF16), own_low)).astype(BF16)
    behind = times(pick_t[...], tail_in[0]).astype(BF16)
    out[...] = times(pick_t[...], home_in[...]) + times(behind, mix)
    for copy in last_sends:
        copy.wait_recv()
    out[...] += times(times(pick_t[...], tail_in[1]).astype(BF16), own_low)
    stores.append(store(out, out_hbm.at[0]))
    for copy in sent + [copy for copies in spread for copy in copies]:
        copy.wait_send()
    for entry, (_, _, _, sections) in enumerate(plan):
        for h in range(pieces):
            only(sections, along(entry, h).wait_send)
    for copy in stores:
        copy.wait()


def hand_on(soft_from, out_from, soft_to, out_to, soft, out, in_sem, out_sem):
    slots = soft.shape[0]
    bands = in_sem.shape[0] - 1
    band = slots // bands
    moves = [
        (soft_from.at[0, pl.ds(i * band, band)], soft.at[pl.ds(i * band, band)], soft_to.at[0, pl.ds(i * band, band)])
        for i in range(bands)
    ] + [(out_from.at[0], out, out_to.at[0])]
    loads = [pltpu.make_async_copy(a, b, in_sem.at[i]) for i, (a, b, _) in enumerate(moves)]
    stores = [pltpu.make_async_copy(b, c, out_sem.at[i]) for i, (_, b, c) in enumerate(moves)]
    for copy in loads:
        copy.start()
    for before, after in zip(loads, stores):
        before.wait()
        after.start()
    for copy in stores:
        copy.wait()


def on_device(enc_rows, proj_weight, row_owner, grad_in, adapter_gain, adapter_down, adapter_up):
    counts = tuple(lax.axis_size(axis) for axis in ("seq", "section", "mp"))
    n_q, n_z, n_m = counts
    _, slots, width = enc_rows.shape
    _, rank, features = adapter_down.shape
    columns = width // n_m
    pieces = 2 if features // n_q % 256 == 0 else 1
    messages = (n_q - 1) + (2 + TICKS) * (n_m - 1) + (1 + TICKS) * n_q + 2
    flops = 2 * slots * features * (width + 3 * rank)
    vmem = pltpu.VMEM
    results = (
        jax.ShapeDtypeStruct((1, slots, features), BF16),
        jax.ShapeDtypeStruct((1, slots, columns), F32),
    )
    soft, enc_grad = pl.pallas_call(
        functools.partial(kernel, counts, pieces),
        out_shape=results,
        in_specs=[pl.BlockSpec(memory_space=pl.ANY)] * 7,
        out_specs=(pl.BlockSpec(memory_space=pl.ANY),) * 2,
        scratch_shapes=[
            vmem((slots, width), BF16),
            vmem((1, slots), jnp.int32),
            vmem((1, features), F32),
            vmem((rank, features), BF16),
            vmem((slots + rank, features), BF16),
            vmem((width + (TICKS + 1) * rank, features), BF16),
            vmem((slots, width), BF16),
            vmem((slots, width), BF16),
            vmem((slots, slots), BF16),
            vmem((slots, features), BF16),
            vmem((n_m, slots + rank, columns), F32),
            vmem((n_m - 1, slots + rank, columns), F32),
            vmem((slots, rank), F32),
            vmem((n_m - 1, slots, rank), F32),
            vmem((TICKS, slots + rank, rank), F32),
            vmem((TICKS, n_m - 1, slots + rank, rank), F32),
            vmem((slots, columns), BF16),
            vmem((slots, columns), BF16),
            vmem((TICKS, slots, rank), BF16),
            vmem((TICKS, slots, rank), BF16),
            vmem((rank, columns), F32),
            vmem((rank, columns), F32),
            vmem((rank, rank), F32),
            vmem((rank, rank), F32),
            vmem((slots, columns), F32),
            pltpu.SemaphoreType.DMA((6 + n_m,)),
            pltpu.SemaphoreType.DMA((features // min(512, features) + 1,)),
            pltpu.SemaphoreType.DMA((messages,)),
            pltpu.SemaphoreType.DMA((messages,)),
            pltpu.SemaphoreType.DMA((2 * TICKS * pieces,)),
            pltpu.SemaphoreType.DMA((TICKS * pieces,)),
            pltpu.SemaphoreType.DMA((TICKS * pieces * (n_q - 1),)),
            pltpu.SemaphoreType.DMA((TICKS * pieces * (n_q - 1),)),
        ],
        compiler_params=pltpu.CompilerParams(
            collective_id=0, has_side_effects=True, vmem_limit_bytes=63 * 1024 * 1024
        ),
        cost_estimate=pl.CostEstimate(flops=flops, bytes_accessed=12 * 1024 * 1024, transcendentals=0),
    )(enc_rows, proj_weight, row_owner, grad_in, adapter_gain, adapter_down, adapter_up)
    return pl.pallas_call(
        hand_on,
        out_shape=results,
        in_specs=[pl.BlockSpec(memory_space=pl.ANY)] * 2,
        out_specs=(pl.BlockSpec(memory_space=pl.ANY),) * 2,
        scratch_shapes=[
            vmem((slots, features), BF16),
            vmem((slots, columns), F32),
            pltpu.SemaphoreType.DMA((9,)),
            pltpu.SemaphoreType.DMA((9,)),
        ],
        compiler_params=pltpu.CompilerParams(vmem_limit_bytes=63 * 1024 * 1024),
        cost_estimate=pl.CostEstimate(flops=0, bytes_accessed=5 * 1024 * 1024, transcendentals=0),
    )(soft, enc_grad)


def solution(mesh):
    placed = (
        P("section", "seq", None),
        P(None, "mp"),
        P("section", "seq"),
        P("section", "seq", "mp"),
        P("section", "mp"),
        P("section", None, "mp"),
        P("section", None, "mp"),
    )
    return jax.shard_map(
        on_device,
        mesh=mesh,
        in_specs=placed,
        out_specs=(P("section", "seq", "mp"), P("section", "seq", "mp")),
        check_vma=False,
    )
```

```python
import functools

import jax
import jax.numpy as jnp
from jax import lax
from jax.experimental import pallas as pl
from jax.experimental.pallas import tpu as pltpu
from jax.sharding import PartitionSpec as P

TICKS = 2
MESH = pl.DeviceIdType.MESH
F32, BF16 = jnp.float32, jnp.bfloat16


def times(a, b):
    return jnp.dot(a, b, preferred_element_type=F32)


def times_t(a, b):
    return lax.dot_general(a, b, (((1,), (1,)), ((), ())), preferred_element_type=F32)


def aligned(value, unit):
    return pl.multiple_of(value, unit)


def kernel(
    counts, pieces,
    enc_hbm, proj_hbm, owner_hbm, grad_hbm, gain_hbm, down_hbm, up_hbm,
    soft_hbm, out_hbm,
    enc, owner, gain, down, x, w, staged, routed, pick_t, soft,
    part, part_in, low, low_in, late, late_in,
    home, home_in, tail, tail_in, q_own, q_in, m_own, m_in, out,
    load_sem, store_sem, send_sem, recv_sem, line_send, line_recv, spread_send, spread_recv,
):
    n_q, n_z, n_m = counts
    q, z, m = lax.axis_index("seq"), lax.axis_index("section"), lax.axis_index("mp")
    slots, width = enc.shape
    rank, features = down.shape
    columns = width // n_m
    per = slots // n_q
    share = features // n_q

    def device(dq, dz, dm):
        return (lax.rem(q + dq % n_q, n_q), lax.rem(z + dz % n_z, n_z), lax.rem(m + dm % n_m, n_m))

    used = [0, 0, 0]
    sent = []

    def load(src, dst):
        copy = pltpu.make_async_copy(src, dst, load_sem.at[used[0]])
        used[0] += 1
        copy.start()
        return copy

    def store(src, dst):
        copy = pltpu.make_async_copy(src, dst, store_sem.at[used[1]])
        used[1] += 1
        copy.start()
        return copy

    def send(src, dst, offsets):
        copy = pltpu.make_async_remote_copy(
            src_ref=src, dst_ref=dst,
            send_sem=send_sem.at[used[2]], recv_sem=recv_sem.at[used[2]],
            device_id=device(*offsets), device_id_type=MESH,
        )
        used[2] += 1
        copy.start()
        sent.append(copy)
        return copy

    owner_load = load(owner_hbm, owner)
    enc_load = load(enc_hbm.at[0], enc)
    low_load = load(up_hbm.at[0], w.at[pl.ds(width, rank)])
    grad_load = load(grad_hbm.at[0], x.at[pl.ds(0, slots)])
    gain_load = load(gain_hbm, gain)
    down_load = load(down_hbm.at[0], down)
    proj_loads = [
        load(proj_hbm.at[pl.ds(j * columns, columns)], w.at[pl.ds(j * columns, columns)])
        for j in range(n_m)
    ]

    targets = {(dq, 0, 0) for dq in range(1, n_q)}
    targets |= {(0, dz % n_z, 0) for dz in (-1, 1)}
    targets |= {(dq, -TICKS % n_z, 0) for dq in range(n_q)}
    targets |= {(0, 0, dm) for dm in range(1, n_m)}
    barrier = pltpu.get_barrier_semaphore()
    for dq, dz, dm in sorted(targets):
        pl.semaphore_signal(barrier, inc=1, device_id=device(-dq, -dz, -dm), device_id_type=MESH)

    pl.semaphore_wait(barrier, len(targets))

    piece = share // pieces
    up_rows = [pl.ds(width + tick * rank, rank) for tick in range(TICKS + 1)]

    def piece_at(h):
        return pl.ds(aligned(q * share + h * piece, 128), piece)

    if n_z == 4 and TICKS == 2:
        plan = [(0, 1, 1, (0, 1, 2)), (0, 2, -2, (2, 3)), (1, 2, 1, (1, 2)), (2, 1, -1, (1,))]
        swapped = z == 0
    else:
        plan = [(tick, tick + 1, 1, None) for tick in range(TICKS)]
        swapped = None

    def only(sections, act):
        if sections is None:
            act()
        else:
            chosen = z == sections[0]
            for section in sections[1:]:
                chosen = jnp.logical_or(chosen, z == section)
            pl.when(chosen)(act)

    def along(entry, h):
        source, slot, dz, _ = plan[entry]
        return pltpu.make_async_remote_copy(
            src_ref=w.at[up_rows[source], piece_at(h)], dst_ref=w.at[up_rows[slot], piece_at(h)],
            send_sem=line_send.at[entry * pieces + h], recv_sem=line_recv.at[(slot - 1) * pieces + h],
            device_id=device(0, dz, 0), device_id_type=MESH,
        )

    def send_from(slot, h):
        for entry, (source, _, _, sections) in enumerate(plan):
            if source == slot:
                only(sections, along(entry, h).start)

    low_load.wait()
    for h in range(pieces):
        send_from(0, h)

    def described(tick, h, dq):
        here = w.at[up_rows[tick + 1], piece_at(h)]
        at = (tick * pieces + h) * (n_q - 1) + dq - 1
        return pltpu.make_async_remote_copy(
            src_ref=here, dst_ref=here, send_sem=spread_send.at[at], recv_sem=spread_recv.at[at],
            device_id=device(dq, 0, 0), device_id_type=MESH,
        )

    spread = [
        [described(tick, h, dq) for h in range(pieces) for dq in range(1, n_q)] for tick in range(TICKS)
    ]

    def pass_slot(tick):
        for h in range(pieces):
            along([slot for _, slot, _, _ in plan].index(tick + 1), h).wait_recv()
            send_from(tick + 1, h)
            for dq in range(1, n_q):
                spread[tick][h * (n_q - 1) + dq - 1].start()

    def pass_on(tick):
        if swapped is None:
            pass_slot(tick)
        else:
            pl.when(swapped)(lambda: pass_slot(TICKS - 1 - tick))
            pl.when(jnp.logical_not(swapped))(lambda: pass_slot(tick))

    owner_load.wait()
    owners = owner[...].astype(F32)
    readers = lax.broadcasted_iota(jnp.int32, (max(8, n_q), slots), 0).astype(F32)
    matches = jnp.where(owners == readers, 1.0, 0.0)
    row_at = lax.broadcasted_iota(jnp.int32, (slots, slots), 0)
    column_at = lax.broadcasted_iota(jnp.int32, (slots, slots), 1)
    earlier = jnp.where(row_at < column_at, 1.0, 0.0).astype(BF16)
    before = times(matches.astype(BF16), earlier)
    order_rank = jnp.sum(matches * before, axis=0, keepdims=True)
    target = jnp.where(owners >= 0.0, owners * per + order_rank, -1.0)
    pick = jnp.where(row_at.astype(F32) == target, 1.0, 0.0)
    enc_load.wait()
    staged[...] = times(pick.astype(BF16), enc[...]).astype(BF16)
    own_rows = pl.ds(aligned(q * per, per), per)

    def rows_of(dq):
        return pl.ds(aligned(lax.rem(q + dq, n_q) * per, per), per)

    enc_sends = [
        send(staged.at[rows_of(dq)], routed.at[own_rows], (dq, 0, 0)) for dq in range(1, n_q)
    ]
    routed[own_rows, :] = staged[own_rows, :]

    pass_on(0)
    pick_t[...] = jnp.transpose(pick).astype(BF16)

    grad_load.wait()
    low[...] = times_t(x[pl.ds(0, slots), :], w[up_rows[0], :])
    low_sends = [send(low, low_in.at[dm - 1], (0, 0, dm)) for dm in range(1, n_m)]
    down_load.wait()
    gain_load.wait()
    x[pl.ds(slots, rank), :] = (gain[...] * down[...].astype(F32)).astype(BF16)
    for tick in range(1, TICKS):
        pass_on(tick)
    for copy in proj_loads:
        copy.wait()
    part_sends = []
    for dm in [*range(1, n_m), 0]:
        block = pl.ds(aligned(lax.rem(m + dm, n_m) * columns, columns), columns)
        part[dm] = times_t(x[...], w[block, :])
        if dm:
            part_sends.append(send(part.at[dm], part_in.at[dm - 1], (0, 0, dm)))

    def share_of(dq):
        return pl.ds(aligned(lax.rem(q + dq, n_q) * share, share), share)

    def late_products(tick):
        rows = up_rows[tick + 1]
        at = share_of(0)
        total = times_t(x[:, at], w[rows, at])
        for dq in range(1, n_q):
            for h in range(pieces):
                spread[tick][h * (n_q - 1) + dq - 1].wait_recv()
            at = share_of(n_q - dq)
            total += times_t(x[:, at], w[rows, at])
        late[tick] = total
        return [send(late.at[tick], late_in.at[tick, dm - 1], (0, 0, dm)) for dm in range(1, n_m)]

    def late_rows(tick, late_sends):
        for copy in late_sends:
            copy.wait_recv()
        sums = late[tick]
        for dm in range(1, n_m):
            sums += late_in[tick, dm - 1]
        tail[tick] = (sums[:slots] + times(u_own, sums[slots:].astype(BF16))).astype(BF16)
        tail_sends = [
            send(tail.at[tick, rows_of(dq)], tail_in.at[tick, own_rows], (dq, -TICKS, 0))
            for dq in range(n_q)
        ]
        return tail_sends, sums[slots:]

    late_sends = late_products(0)
    for copy in low_sends + part_sends:
        copy.wait_recv()
    u_own = low[...]
    sums = part[0]
    for dm in range(1, n_m):
        u_own += low_in[dm - 1]
        sums += part_in[dm - 1]
    u_own = u_own.astype(BF16)
    q_own[...] = sums[slots:]
    q_send = send(q_own, q_in, (0, -1, 0))
    home[...] = (sums[:slots] + times(u_own, sums[slots:].astype(BF16))).astype(BF16)
    home_sends = [
        send(home.at[rows_of(dq)], home_in.at[own_rows], (dq, -TICKS, 0)) for dq in range(n_q)
    ]
    tail_sends, low_mix = late_rows(0, late_sends)
    m_own[...] = low_mix
    m_send = send(m_own, m_in, (0, -1, 0))

    for copy in enc_sends:
        copy.wait_recv()
    stores = []
    tile = min(512, features)

    def soft_tokens(tiles):
        for t in tiles:
            at = pl.ds(t * tile, tile)
            soft[:, at] = times(routed[...], w[pl.ds(0, width), at]).astype(BF16)
            stores.append(store(soft.at[:, at], soft_hbm.at[0, :, at]))

    n_tiles = features // tile
    soft_tokens(range(n_tiles))
    late_sends = late_products(1)
    last_sends, _ = late_rows(1, late_sends)

    for copy in home_sends + [q_send, m_send] + tail_sends:
        copy.wait_recv()
    own_low = q_own[...].astype(BF16)
    mix = (q_in[...] + times(m_in[...].astype(BF16), own_low)).astype(BF16)
    behind = times(pick_t[...], tail_in[0]).astype(BF16)
    out[...] = times(pick_t[...], home_in[...]) + times(behind, mix)
    for copy in last_sends:
        copy.wait_recv()
    out[...] += times(times(pick_t[...], tail_in[1]).astype(BF16), own_low)
    stores.append(store(out, out_hbm.at[0]))
    for copy in sent + [copy for copies in spread for copy in copies]:
        copy.wait_send()
    for entry, (_, _, _, sections) in enumerate(plan):
        for h in range(pieces):
            only(sections, along(entry, h).wait_send)
    for copy in stores:
        copy.wait()


def hand_on(soft_from, out_from, soft_to, out_to, soft, out, in_sem, out_sem):
    slots = soft.shape[0]
    bands = in_sem.shape[0] - 1
    band = slots // bands
    moves = [
        (soft_from.at[0, pl.ds(i * band, band)], soft.at[pl.ds(i * band, band)], soft_to.at[0, pl.ds(i * band, band)])
        for i in range(bands)
    ] + [(out_from.at[0], out, out_to.at[0])]
    loads = [pltpu.make_async_copy(a, b, in_sem.at[i]) for i, (a, b, _) in enumerate(moves)]
    stores = [pltpu.make_async_copy(b, c, out_sem.at[i]) for i, (_, b, c) in enumerate(moves)]
    for copy in loads:
        copy.start()
    for before, after in zip(loads, stores):
        before.wait()
        after.start()
    for copy in stores:
        copy.wait()


def on_device(enc_rows, proj_weight, row_owner, grad_in, adapter_gain, adapter_down, adapter_up):
    counts = tuple(lax.axis_size(axis) for axis in ("seq", "section", "mp"))
    n_q, n_z, n_m = counts
    _, slots, width = enc_rows.shape
    _, rank, features = adapter_down.shape
    columns = width // n_m
    pieces = 2 if features // n_q % 256 == 0 else 1
    messages = (n_q - 1) + (2 + TICKS) * (n_m - 1) + (1 + TICKS) * n_q + 2
    flops = 2 * slots * features * (width + 3 * rank)
    vmem = pltpu.VMEM
    results = (
        jax.ShapeDtypeStruct((1, slots, features), BF16),
        jax.ShapeDtypeStruct((1, slots, columns), F32),
    )
    soft, enc_grad = pl.pallas_call(
        functools.partial(kernel, counts, pieces),
        out_shape=results,
        in_specs=[pl.BlockSpec(memory_space=pl.ANY)] * 7,
        out_specs=(pl.BlockSpec(memory_space=pl.ANY),) * 2,
        scratch_shapes=[
            vmem((slots, width), BF16),
            vmem((1, slots), jnp.int32),
            vmem((1, features), F32),
            vmem((rank, features), BF16),
            vmem((slots + rank, features), BF16),
            vmem((width + (TICKS + 1) * rank, features), BF16),
            vmem((slots, width), BF16),
            vmem((slots, width), BF16),
            vmem((slots, slots), BF16),
            vmem((slots, features), BF16),
            vmem((n_m, slots + rank, columns), F32),
            vmem((n_m - 1, slots + rank, columns), F32),
            vmem((slots, rank), F32),
            vmem((n_m - 1, slots, rank), F32),
            vmem((TICKS, slots + rank, rank), F32),
            vmem((TICKS, n_m - 1, slots + rank, rank), F32),
            vmem((slots, columns), BF16),
            vmem((slots, columns), BF16),
            vmem((TICKS, slots, rank), BF16),
            vmem((TICKS, slots, rank), BF16),
            vmem((rank, columns), F32),
            vmem((rank, columns), F32),
            vmem((rank, rank), F32),
            vmem((rank, rank), F32),
            vmem((slots, columns), F32),
            pltpu.SemaphoreType.DMA((6 + n_m,)),
            pltpu.SemaphoreType.DMA((features // min(512, features) + 1,)),
            pltpu.SemaphoreType.DMA((messages,)),
            pltpu.SemaphoreType.DMA((messages,)),
            pltpu.SemaphoreType.DMA((2 * TICKS * pieces,)),
            pltpu.SemaphoreType.DMA((TICKS * pieces,)),
            pltpu.SemaphoreType.DMA((TICKS * pieces * (n_q - 1),)),
            pltpu.SemaphoreType.DMA((TICKS * pieces * (n_q - 1),)),
        ],
        compiler_params=pltpu.CompilerParams(
            collective_id=0, has_side_effects=True, vmem_limit_bytes=63 * 1024 * 1024
        ),
        cost_estimate=pl.CostEstimate(flops=flops, bytes_accessed=12 * 1024 * 1024, transcendentals=0),
    )(enc_rows, proj_weight, row_owner, grad_in, adapter_gain, adapter_down, adapter_up)
    return pl.pallas_call(
        hand_on,
        out_shape=results,
        in_specs=[pl.BlockSpec(memory_space=pl.ANY)] * 2,
        out_specs=(pl.BlockSpec(memory_space=pl.ANY),) * 2,
        scratch_shapes=[
            vmem((slots, features), BF16),
            vmem((slots, columns), F32),
            pltpu.SemaphoreType.DMA((9,)),
            pltpu.SemaphoreType.DMA((9,)),
        ],
        compiler_params=pltpu.CompilerParams(vmem_limit_bytes=63 * 1024 * 1024),
        cost_estimate=pl.CostEstimate(flops=0, bytes_accessed=5 * 1024 * 1024, transcendentals=0),
    )(soft, enc_grad)


def solution(mesh):
    placed = (
        P("section", "seq", None),
        P(None, "mp"),
        P("section", "seq"),
        P("section", "seq", "mp"),
        P("section", "mp"),
        P("section", None, "mp"),
        P("section", None, "mp"),
    )
    return jax.shard_map(
        on_device,
        mesh=mesh,
        in_specs=placed,
        out_specs=(P("section", "seq", "mp"), P("section", "seq", "mp")),
        check_vma=False,
    )
```
